128 devices in a mesh: row: 8 (over y_hi, x), col: 16 (over y_lo, z, core).
Axes of the slice: x: 4, y: 4 (y_hi: 2, y_lo: 2; y = y_hi * 2 + y_lo), z: 4, core: 2. Of those that a mesh axis runs over, the one named last changes fastest.
Arguments:
- trailing_grad: bfloat16 [8, 16, 192, 24576], P(None, 'col', None, 'row'), may hold values from -6 to 6
- panel: bfloat16 [24576, 512], P(('row', 'col')), may hold values from -0.0390625 to 0.0390625
- panel_grad: float32 [24576, 512], P(('row', 'col')), may hold values from -6 to 6
- diag_factor: float32 [512, 512], replicated, may hold values from -2 to 2, as said below
- diag_grad: float32 [512, 512], replicated, may hold values from -6 to 6
Outputs:
- panel_adj: float32 [24576, 512], P(('row', 'col'))
- diag_adj: float32 [512, 512], replicated
The draws below stay inside these ranges and needn't reach their ends.
Inputs may be any that keep to these rules, and one draw needn't show every extreme that they name: `diag_factor`: lower triangular with zeros above the diagonal; diagonal entries between 1 and 2.
All inputs are finite; a program needn't handle non-finite values.
Results may differ from the reference program's by a relative error of at most 0.0003.
Values may be sent and summed in bfloat16 or wider, within the bound.
No kernel may reach another device: no remote copies, remote signals or barrier semaphores. Data moves between devices by JAX's collectives and lax.ppermute only.
A program may use at most 64 MiB of HBM per device.

```python
import jax
import jax.numpy as jnp
from jax import lax

M = 24576
B = 512
GROUP = 192
N_ROW = 8
N_COL = 16


def draw_diag_factor(key, part):
    base = jax.random.fold_in(key, 7)
    key_diag, key_off = jax.random.split(base)
    diagonal = jax.random.uniform(key_diag, (B,), jnp.float32, 1.0, 2.0)
    off = jax.random.normal(key_off, (B, B), jnp.float32)
    off = jnp.clip(off * (0.6 / jnp.sqrt(B * 1.0)), -1.0, 1.0)
    rows = lax.broadcasted_iota(jnp.int32, (B, B), 0)
    cols = lax.broadcasted_iota(jnp.int32, (B, B), 1)
    strict = jnp.where(rows > cols, off, 0.0)
    return strict + jnp.diag(diagonal)


def strengthened(values, key, source, target, parts, factor):
    def block_of(dim):
        return (jnp.arange(values.shape[dim]) // (values.shape[dim] // parts)).reshape((-1,) + (1,) * (values.ndim - 1 - dim))

    one_side = jax.random.permutation(key, parts)[block_of(target)]
    second = (block_of(target) + parts // 2) % parts
    return jnp.where((block_of(source) == one_side) | (block_of(source) == second), factor * values, values)


def steps_of(rng, shape, shards, low, top_value):
    loudness, own = 1.0, jax.random.fold_in(rng, 6)
    for axis_at, parts in shards:
        steps = jnp.exp(jax.random.uniform(jax.random.fold_in(own, axis_at), (parts,), jnp.float32, low / len(shards), top_value / len(shards)))
        loudness = loudness * jnp.repeat(steps, shape[axis_at] // parts).reshape([-1 if axis == axis_at else 1 for axis in range(len(shape))])
    return loudness


def centred(stream_key, extent, deviation, most, pieces=(), held_as=jnp.bfloat16):
    array = jax.random.normal(stream_key, extent, jnp.float32) * deviation
    if len(pieces) > 0:
        array = steps_of(stream_key, extent, pieces, -0.22, 0.18) * array
    return jnp.clip(array, min=-most, max=most).astype(held_as)


def noise_with(rng, shape, spread, most, cuts, heavy, kind=jnp.bfloat16):
    entries = spread * jax.random.normal(rng, shape, jnp.float32)
    if cuts:
        entries = entries * steps_of(rng, shape, cuts, -0.22, 0.18)
    return jnp.clip(strengthened(entries, jax.random.fold_in(rng, 3), *heavy), -most, most).astype(kind)


def setup_inputs(seed: int = 0) -> dict:
    key_of = jax.random.split(jax.random.key(seed), 6)
    return {
        "trailing_grad": noise_with(key_of[0], (N_ROW, N_COL, GROUP, M), 1.0, 6.0, ((1, 16), (3, 8)), (1, 3, 16, 2.0)),
        "panel": centred(key_of[1], (M, B), M ** -0.5, 0.0390625, ((0, 128),)),
        "panel_grad": centred(key_of[2], (M, B), 1.0, 6.0, ((0, 128),), jnp.float32),
        "diag_factor": draw_diag_factor(jax.random.fold_in(key_of[5], 71), 0),
        "diag_grad": centred(key_of[4], (B, B), 1.0, 6.0, (), jnp.float32),
    }


def halve_lower(matrix):
    rows = lax.broadcasted_iota(jnp.int32, matrix.shape, 0)
    cols = lax.broadcasted_iota(jnp.int32, matrix.shape, 1)
    keep = jnp.where(rows > cols, 1.0, jnp.where(rows == cols, 0.5, 0.0)).astype(matrix.dtype)
    return matrix * keep

def adjoint_block(diag_new, lower):
    inner = halve_lower(jnp.dot(lower.T, jnp.tril(diag_new), precision=lax.Precision.HIGHEST))
    left = jax.scipy.linalg.solve_triangular(lower, inner, lower=True, trans=1)
    right = jax.scipy.linalg.solve_triangular(lower, left.T, lower=True, trans=1).T
    return 0.5 * (right + right.T)

def reference(trailing_grad, panel, panel_grad, diag_factor, diag_grad):
    flipped = trailing_grad.reshape(M, M)
    direct = lax.dot_general(flipped.astype(jnp.float32), panel.astype(jnp.float32), (((0,), (0,)), ((), ())), preferred_element_type=jnp.float32)
    transposed = jnp.dot(flipped.astype(jnp.float32), panel.astype(jnp.float32), preferred_element_type=jnp.float32)
    reduced = panel_grad - direct - transposed
    lower = jnp.tril(diag_factor)
    panel_adj = jax.scipy.linalg.solve_triangular(lower, reduced.T, lower=True, trans=1).T
    contrib = lax.dot_general(panel_adj, panel.astype(jnp.float32), (((0,), (0,)), ((), ())), precision=lax.Precision.HIGHEST)
    diag_new = diag_grad - contrib
    return (panel_adj, adjoint_block(diag_new, lower))
```

```python
import functools

import jax
import jax.numpy as jnp
from jax import lax
from jax.experimental import pallas as pl
from jax.experimental.pallas import tpu as pltpu
from jax.sharding import Mesh, PartitionSpec as P

f32 = jnp.float32
bf16 = jnp.bfloat16
U = 192
B = 512
BLK = 128
NB = B // BLK
LOWER = [(i, j) for i in range(NB) for j in range(i + 1)]
CH = len(LOWER) * BLK // 8
VMEM_LIMIT = 60 * 1024 * 1024


def whole():
    return pl.BlockSpec(memory_space=pltpu.VMEM)


def params(**kw):
    return pltpu.CompilerParams(vmem_limit_bytes=VMEM_LIMIT, **kw)


def hi_dot(a, b, dims):
    return lax.dot_general(
        a, b, (dims, ((), ())), precision=lax.Precision.HIGHEST, preferred_element_type=f32
    )


def shift(x, axis, k, n=4):
    return lax.ppermute(x, axis, [(i, (i + k) % n) for i in range(n)])


def iotas(n):
    return (
        lax.broadcasted_iota(jnp.int32, (n, n), 0),
        lax.broadcasted_iota(jnp.int32, (n, n), 1),
    )


def block(ref, i, j):
    return ref[i * BLK : (i + 1) * BLK, j * BLK : (j + 1) * BLK]


def prep_kernel(l_ref, pg_ref, p_ref, inv_ref, g_ref):
    rows, cols = iotas(BLK)
    blocks = []
    inv = []
    for b in range(NB):
        m = jnp.where(rows >= cols, block(l_ref, b, b), 0.0)
        blocks.append(m)
        inv.append(jnp.where(rows == cols, 1.0 / jnp.where(rows == cols, m, 1.0), 0.0))
    s = 1
    while s < BLK:
        sel = (rows // s != cols // s) & (rows // (2 * s) == cols // (2 * s))
        right = [hi_dot(jnp.where(sel, blocks[b], 0.0), inv[b], ((1,), (0,))) for b in range(NB)]
        inv = [inv[b] - hi_dot(inv[b], right[b], ((1,), (0,))) for b in range(NB)]
        s *= 2
    for b in range(NB):
        inv_ref[b] = inv[b]
    p = p_ref[...]
    g = pg_ref[...]
    total = None
    for _ in range(3):
        part = g.astype(bf16)
        g = g - part.astype(f32)
        term = lax.dot_general(part, p, (((0,), (0,)), ((), ())), preferred_element_type=f32)
        total = term if total is None else total + term
    g_ref[...] = total


def prep(lower, panel_grad, panel):
    return pl.pallas_call(
        prep_kernel,
        out_shape=(
            jax.ShapeDtypeStruct((NB, BLK, BLK), f32),
            jax.ShapeDtypeStruct((B, B), f32),
        ),
        in_specs=[whole()] * 3,
        out_specs=(whole(), whole()),
        compiler_params=params(),
        cost_estimate=pl.CostEstimate(flops=4_000_000_000, bytes_accessed=3_000_000, transcendentals=0),
        name="prep",
    )(lower, panel_grad, panel)


def direct_kernel(s_ref, f_ref, own, swp, r1, r2, r3, *refs):
    mine = refs[:4]
    other, pc = refs[4], refs[5]
    step = pl.program_id(0)
    x, yh, c = s_ref[8], s_ref[9], s_ref[10]

    @pl.when(step == 0)
    def _():
        def put(a, val):
            pc[pl.ds(pl.multiple_of(a * U, U), U), :] = val

        put(yh * 4 + x, own[...])
        put((1 - yh) * 4 + x, swp[...])
        for k, r in ((1, r1), (2, r2), (3, r3)):
            xs = lax.rem(x + 4 - k, 4)
            put(yh * 4 + xs, r[0])
            put((1 - yh) * 4 + xs, r[1])

    d = lax.dot_general(f_ref[...], pc[...], (((0,), (0,)), ((), ())), preferred_element_type=f32)
    lo, hi = d[:U], d[U:]
    first = c == 0
    keep = jnp.where(first, lo, hi)
    give = jnp.where(first, hi, lo)
    for k in range(4):
        for m in range(2):

            @pl.when(step == 2 * k + m)
            def _():
                mine[k][m] = keep
                other[k, m] = give


def direct(scalars, flip, own, swp, recv):
    grid_spec = pltpu.PrefetchScalarGridSpec(
        num_scalar_prefetch=1,
        grid=(8,),
        in_specs=[pl.BlockSpec((8 * U, 2 * U), lambda i, s: (0, s[i]))] + [whole()] * 5,
        out_specs=[whole()] * 5,
        scratch_shapes=[pltpu.VMEM((8 * U, B), bf16)],
    )
    out = pl.pallas_call(
        direct_kernel,
        grid_spec=grid_spec,
        out_shape=[jax.ShapeDtypeStruct((2, U, B), f32)] * 4
        + [jax.ShapeDtypeStruct((4, 2, U, B), f32)],
        compiler_params=params(),
        cost_estimate=pl.CostEstimate(flops=4_831_838_208, bytes_accessed=17_000_000, transcendentals=0),
        name="direct",
    )(scalars, flip, own, swp, *recv)
    return out[:4], out[4]


def transposed_kernel(s_ref, f0, f1, *refs):
    zown, zr, pown, prr = refs[0:2], refs[2:5], refs[5], refs[6:9]
    cown, cswp, c1, c2, c3 = refs[9:14]
    outs = refs[14:18]
    st_ref, pr, pc = refs[18], refs[19], refs[20]
    step = pl.program_id(0)
    z, yl, c = s_ref[8], s_ref[9], s_ref[10]
    x, yh = s_ref[11], s_ref[12]

    @pl.when(step == 0)
    def _():
        def put(yb, zb, cb, val):
            n = ((yb * 4 + zb) * 2 + cb) * U
            pr[pl.ds(pl.multiple_of(n, U), U), :] = val

        put(yl, z, c, zown[0][...])
        put(1 - yl, z, c, zown[1][...])
        put(yl, z, 1 - c, pown[0])
        put(1 - yl, z, 1 - c, pown[1])
        for k in (1, 2, 3):
            zs = lax.rem(z + 4 - k, 4)
            for m, yb in ((0, yl), (1, 1 - yl)):
                put(yb, zs, c, zr[k - 1][m])
                put(yb, zs, 1 - c, prr[k - 1][m])
        pc[0:U, :] = cown[...]
        pc[U : 2 * U, :] = cswp[...]
        for k, r in ((1, c3), (2, c2), (3, c1)):
            pc[2 * k * U : (2 * k + 1) * U, :] = r[0]
            pc[(2 * k + 1) * U : (2 * k + 2) * U, :] = r[1]
        st_ref[...] = jnp.zeros_like(st_ref)

    f = jnp.concatenate([f0[...], f1[...]], axis=0)
    t = jnp.dot(f, pr[...], preferred_element_type=f32)
    for k in range(4):

        @pl.when(step == k)
        def _():
            outs[k][0] = t[:U]
            outs[k][1] = t[U:]

    hi = t.astype(bf16)
    lo = (t - hi.astype(f32)).astype(bf16)
    p = pc[pl.ds(pl.multiple_of(step * 2 * U, 2 * U), 2 * U), :]
    dims = (((0,), (0,)), ((), ()))
    st_ref[...] += lax.dot_general(p, hi, dims, preferred_element_type=f32) + lax.dot_general(
        p, lo, dims, preferred_element_type=f32
    )


def transposed(scalars, flip, zown, zr, pown, prr, cpanel):
    grid_spec = pltpu.PrefetchScalarGridSpec(
        num_scalar_prefetch=1,
        grid=(4,),
        in_specs=[
            pl.BlockSpec((U, 16 * U), lambda i, s: (s[2 * i], 0)),
            pl.BlockSpec((U, 16 * U), lambda i, s: (s[2 * i + 1], 0)),
        ]
        + [whole()] * 14,
        out_specs=[whole()] * 5,
        scratch_shapes=[pltpu.VMEM((16 * U, B), bf16), pltpu.VMEM((8 * U, B), bf16)],
    )
    out = pl.pallas_call(
        transposed_kernel,
        grid_spec=grid_spec,
        out_shape=[jax.ShapeDtypeStruct((2, U, B), f32)] * 4 + [jax.ShapeDtypeStruct((B, B), f32)],
        compiler_params=params(),
        cost_estimate=pl.CostEstimate(flops=6_500_000_000, bytes_accessed=17_000_000, transcendentals=0),
        name="transposed",
    )(scalars, flip, flip, *zown, *zr, pown, *prr, *cpanel)
    return out[:4], out[4]


def pack_kernel(s_ref, g_ref, st_ref, *refs):
    mine, other, flat = refs[:4], refs[4], refs[5]
    c, y = s_ref[0], s_ref[1]
    for n, (i, j) in enumerate(LOWER):
        flat[n * BLK : (n + 1) * BLK, :] = block(g_ref, i, j) - block(st_ref, i, j) - block(st_ref, j, i).T
    for k in range(4):
        q = lax.rem(y + k, 4)
        mine[k][...] = flat[pl.ds(pl.multiple_of((c * 4 + q) * CH, CH), CH), :]
        other[k] = flat[pl.ds(pl.multiple_of(((1 - c) * 4 + q) * CH, CH), CH), :]


def pack(scalars, g, st):
    out = pl.pallas_call(
        pack_kernel,
        out_shape=[jax.ShapeDtypeStruct((CH, BLK), f32)] * 4 + [jax.ShapeDtypeStruct((4, CH, BLK), f32)],
        in_specs=[pl.BlockSpec(memory_space=pltpu.SMEM)] + [whole()] * 2,
        out_specs=[whole()] * 5,
        scratch_shapes=[pltpu.VMEM((8 * CH, BLK), f32)],
        compiler_params=params(),
        cost_estimate=pl.CostEstimate(flops=2_000_000, bytes_accessed=3_000_000, transcendentals=0),
        name="pack",
    )(scalars, g, st)
    return out[:4], out[4]


def tail_kernel(s_ref, mine, other, l_ref, inv_ref, dg_ref, out_ref, flat):
    c, y = s_ref[0], s_ref[1]
    for k in range(4):
        q = lax.rem(y + 4 - k, 4)
        flat[pl.ds(pl.multiple_of((c * 4 + q) * CH, CH), CH), :] = mine[k]
        flat[pl.ds(pl.multiple_of(((1 - c) * 4 + q) * CH, CH), CH), :] = other[k]
    rows, cols = iotas(BLK)
    low = {(i, j): block(l_ref, i, j) for (i, j) in LOWER}
    for i in range(NB):
        low[i, i] = jnp.where(rows >= cols, low[i, i], 0.0)
    q = {ij: flat[n * BLK : (n + 1) * BLK, :] for n, ij in enumerate(LOWER)}
    tdot = functools.partial(hi_dot, dims=((0,), (0,)))
    ndot = functools.partial(hi_dot, dims=((1,), (0,)))
    con = {}
    for j in range(NB):
        for i in reversed(range(j, NB)):
            acc = q[i, j]
            for k in range(i + 1, NB):
                acc = acc - tdot(low[k, i], con[k, j])
            con[i, j] = tdot(inv_ref[i], acc)
    new = {ij: block(dg_ref, *ij) - con[ij] for ij in LOWER}
    for i in range(NB):
        new[i, i] = jnp.where(rows >= cols, new[i, i], 0.0)
    inner = {}
    for i, j in LOWER:
        acc = tdot(low[i, i], new[i, j])
        for k in range(i + 1, NB):
            acc = acc + tdot(low[k, i], new[k, j])
        if i == j:
            acc = acc * jnp.where(rows > cols, 1.0, jnp.where(rows == cols, 0.5, 0.0))
        inner[i, j] = acc
    left = {}
    for i in reversed(range(NB)):
        acc = jnp.concatenate([inner.get((i, j), jnp.zeros((BLK, BLK), f32)) for j in range(NB)], axis=1)
        for k in range(i + 1, NB):
            acc = acc - tdot(low[k, i], left[k])
        left[i] = tdot(inv_ref[i], acc)
    left = jnp.concatenate([left[i] for i in range(NB)], axis=0)
    right = {}
    for j in reversed(range(NB)):
        acc = left[:, j * BLK : (j + 1) * BLK]
        for k in range(j + 1, NB):
            acc = acc - ndot(right[k], low[k, j])
        right[j] = ndot(acc, inv_ref[j])
    for i in range(NB):
        for j in range(i + 1):
            a = right[j][i * BLK : (i + 1) * BLK]
            b = right[i][j * BLK : (j + 1) * BLK]
            v = 0.5 * (a + b.T)
            out_ref[i * BLK : (i + 1) * BLK, j * BLK : (j + 1) * BLK] = v
            if i != j:
                out_ref[j * BLK : (j + 1) * BLK, i * BLK : (i + 1) * BLK] = v.T


def tail(scalars, mine, other, lower, inv, diag_grad):
    return pl.pallas_call(
        tail_kernel,
        out_shape=jax.ShapeDtypeStruct((B, B), f32),
        in_specs=[pl.BlockSpec(memory_space=pltpu.SMEM)] + [whole()] * 5,
        out_specs=whole(),
        scratch_shapes=[pltpu.VMEM((8 * CH, BLK), f32)],
        compiler_params=params(),
        cost_estimate=pl.CostEstimate(flops=6_000_000_000, bytes_accessed=5_000_000, transcendentals=0),
        name="tail",
    )(scalars, mine, other, lower, inv, diag_grad)


def solve_kernel(r_ref, d_ref, t_ref, l_ref, inv_ref, out_ref):
    r = r_ref[...] - d_ref[...] - t_ref[...]
    xs = {}
    for j in reversed(range(NB)):
        acc = r[:, j * BLK : (j + 1) * BLK]
        for k in range(j + 1, NB):
            acc = acc - hi_dot(xs[k], block(l_ref, k, j), ((1,), (0,)))
        xs[j] = hi_dot(acc, inv_ref[j], ((1,), (0,)))
        out_ref[:, j * BLK : (j + 1) * BLK] = xs[j]


def solve(r, d, t, lower, inv):
    return pl.pallas_call(
        solve_kernel,
        out_shape=jax.ShapeDtypeStruct((U, B), f32),
        in_specs=[whole()] * 5,
        out_specs=whole(),
        compiler_params=params(),
        cost_estimate=pl.CostEstimate(flops=1_000_000_000, bytes_accessed=3_000_000, transcendentals=0),
        name="solve",
    )(r, d, t, lower, inv)


def on_device(trailing_grad, panel, panel_grad, diag_factor, diag_grad):
    flip = trailing_grad.reshape(-1, trailing_grad.shape[3])
    x, yh = lax.axis_index("x"), lax.axis_index("yh")
    z, yl, c = lax.axis_index("z"), lax.axis_index("yl"), lax.axis_index("c")
    y = yh * 2 + yl
    ints = lambda *v: jnp.stack([jnp.asarray(e, jnp.int32) for e in v])
    d_scal = ints(*[(yl ^ m) * 4 + (z + k) % 4 for k in range(4) for m in range(2)], x, yh, c)
    t_scal = ints(*[(yh ^ m) * 4 + (x + k) % 4 for k in range(4) for m in range(2)], z, yl, c, x, yh)
    cy = ints(c, y)

    x_swp = shift(panel, "yh", 1, 2)
    z_swp = shift(panel, "yl", 1, 2)
    x_two = jnp.stack([panel, x_swp])
    z_two = jnp.stack([panel, z_swp])
    x_recv = [None] * 4
    z_recv = [None] * 4
    for k in (2, 1, 3):
        x_recv[k] = shift(x_two, "x", k)
    for k in (2, 1, 3):
        z_recv[k] = shift(z_two, "z", k)
    pair_own = shift(z_two, "c", 1, 2)
    pair_recv = [None] + [shift(z_recv[k], "c", 1, 2) for k in (1, 2, 3)]
    inv, g = prep(diag_factor, panel_grad, panel)

    d_mine, d_other = direct(d_scal, flip, panel, x_swp, x_recv[1:])
    d_pair = shift(d_other, "c", 1, 2)
    t_own, st = transposed(
        t_scal, flip, (panel, z_swp), z_recv[1:], pair_own, pair_recv[1:], (panel, x_swp, *x_recv[1:])
    )

    t_in = [None] * 4
    for k in (2, 1, 3):
        t_in[k] = shift(t_own[k], "x", k)
    d_sum = [d_mine[k] + d_pair[k] for k in range(4)]
    d_in = [None] * 4
    for k in (2, 1, 3):
        d_in[k] = shift(d_sum[k], "z", k)
    t_far = t_own[0][1] + t_in[1][1] + t_in[2][1] + t_in[3][1]
    d_far = d_sum[0][1] + d_in[1][1] + d_in[2][1] + d_in[3][1]
    t_last = shift(t_far, "yh", 1, 2)
    d_last = shift(d_far, "yl", 1, 2)
    near = (
        panel_grad
        - (t_own[0][0] + t_in[1][0] + t_in[2][0] + t_in[3][0])
        - (d_sum[0][0] + d_in[1][0] + d_in[2][0] + d_in[3][0])
    )
    panel_adj = solve(near, d_last, t_last, diag_factor, inv)

    q_mine, q_other = pack(cy, g, st)
    q_pair = shift(q_other, "c", 1, 2)
    q = [q_mine[k] + q_pair[k] for k in range(4)]
    q_in = [shift(q[k], ("yh", "yl"), k) for k in (1, 2, 3)]
    part = q[0] + q_in[0] + q_in[1] + q_in[2]
    for axis in ("z", "x"):
        got = [shift(part, axis, k) for k in (1, 2, 3)]
        part = (part + got[1]) + (got[0] + got[2])
    q_all = jnp.stack([part] + [shift(part, ("yh", "yl"), k) for k in (1, 2, 3)])
    diag_adj = tail(cy, q_all, shift(q_all, "c", 1, 2), diag_factor, inv, diag_grad)
    return panel_adj, diag_adj


def solution(mesh):
    fine = Mesh(mesh.devices.reshape(2, 4, 2, 4, 2), ("yh", "x", "yl", "z", "c"))
    row, col = ("yh", "x"), ("yl", "z", "c")
    return jax.shard_map(
        on_device,
        mesh=fine,
        in_specs=(P(None, col, None, row), P(row + col, None), P(row + col, None), P(), P()),
        out_specs=(P(row + col, None), P()),
        check_vma=False,
    )
```

```python
import functools

import jax
import jax.numpy as jnp
from jax import lax
from jax.experimental import pallas as pl
from jax.experimental.pallas import tpu as pltpu
from jax.sharding import Mesh, PartitionSpec as P

f32 = jnp.float32
bf16 = jnp.bfloat16
f16 = jnp.float16
U = 192
B = 512
BLK = 128
NB = B // BLK
LOWER = [(i, j) for i in range(NB) for j in range(i + 1)]
CH = len(LOWER) * BLK // 8
VMEM_LIMIT = 60 * 1024 * 1024


def whole():
    return pl.BlockSpec(memory_space=pltpu.VMEM)


def params(**kw):
    return pltpu.CompilerParams(vmem_limit_bytes=VMEM_LIMIT, **kw)


def hi_dot(a, b, dims):
    return lax.dot_general(
        a, b, (dims, ((), ())), precision=lax.Precision.HIGHEST, preferred_element_type=f32
    )


def shift(x, axis, k, n=4):
    return lax.ppermute(x, axis, [(i, (i + k) % n) for i in range(n)])


def iotas(n):
    return (
        lax.broadcasted_iota(jnp.int32, (n, n), 0),
        lax.broadcasted_iota(jnp.int32, (n, n), 1),
    )


def block(ref, i, j):
    return ref[i * BLK : (i + 1) * BLK, j * BLK : (j + 1) * BLK]


def prep_kernel(l_ref, pg_ref, p_ref, inv_ref, g_ref):
    rows, cols = iotas(BLK)
    blocks = []
    inv = []
    for b in range(NB):
        m = jnp.where(rows >= cols, block(l_ref, b, b), 0.0)
        blocks.append(m)
        inv.append(jnp.where(rows == cols, 1.0 / jnp.where(rows == cols, m, 1.0), 0.0))
    s = 1
    while s < BLK:
        sel = (rows // s != cols // s) & (rows // (2 * s) == cols // (2 * s))
        right = [hi_dot(jnp.where(sel, blocks[b], 0.0), inv[b], ((1,), (0,))) for b in range(NB)]
        inv = [inv[b] - hi_dot(inv[b], right[b], ((1,), (0,))) for b in range(NB)]
        s *= 2
    for b in range(NB):
        inv_ref[b] = inv[b]
    p = p_ref[...]
    g = pg_ref[...]
    total = None
    for _ in range(3):
        part = g.astype(bf16)
        g = g - part.astype(f32)
        term = lax.dot_general(part, p, (((0,), (0,)), ((), ())), preferred_element_type=f32)
        total = term if total is None else total + term
    g_ref[...] = total


def prep(lower, panel_grad, panel):
    return pl.pallas_call(
        prep_kernel,
        out_shape=(
            jax.ShapeDtypeStruct((NB, BLK, BLK), f32),
            jax.ShapeDtypeStruct((B, B), f32),
        ),
        in_specs=[whole()] * 3,
        out_specs=(whole(), whole()),
        compiler_params=params(),
        cost_estimate=pl.CostEstimate(flops=4_000_000_000, bytes_accessed=3_000_000, transcendentals=0),
        name="prep",
    )(lower, panel_grad, panel)


DIM0 = (((0,), (0,)), ((), ()))
ANY = pl.BlockSpec(memory_space=pl.ANY)


def band(ref, i):
    return ref.at[pl.ds(pl.multiple_of(i * U, U), U), :]


def pair_kernel(p, xs, zs, *refs):
    x_two, z_two, sem = refs[-3:]
    jobs = [(p, x_two.at[0]), (p, z_two.at[0]), (xs, x_two.at[1]), (zs, z_two.at[1])]
    copies = [pltpu.make_async_copy(a, b, sem.at[i]) for i, (a, b) in enumerate(jobs)]
    for cp in copies:
        cp.start()
    for cp in copies:
        cp.wait()


def pair(p, xs, zs, *after):
    return pl.pallas_call(
        pair_kernel,
        out_shape=[jax.ShapeDtypeStruct((2, U, B), bf16)] * 2,
        in_specs=[ANY] * (3 + len(after)),
        out_specs=[ANY] * 2,
        scratch_shapes=[pltpu.SemaphoreType.DMA((4,))],
        compiler_params=params(),
        cost_estimate=pl.CostEstimate(flops=0, bytes_accessed=1_600_000, transcendentals=0),
        name="pair",
    )(p, xs, zs, *after)


def direct_kernel(s_ref, f_ref, own, swp, r1, r2, r3, *refs):
    refs = refs[-10:]
    mine, other, pc, keep, give, s_in, s_out = refs[:4], *refs[4:]
    step = pl.program_id(0)
    x, yh, c = s_ref[8], s_ref[9], s_ref[10]
    copies = []
    for k in range(4):
        copies.append(
            (
                pltpu.make_async_copy(keep.at[k], mine[k], s_out.at[k]),
                pltpu.make_async_copy(give.at[k], other.at[k], s_out.at[4 + k]),
            )
        )

    @pl.when(step == 0)
    def _():
        jobs = [(yh * 4 + x, own), ((1 - yh) * 4 + x, swp)]
        for k, r in ((1, r1), (2, r2), (3, r3)):
            xs = lax.rem(x + 4 - k, 4)
            jobs += [(yh * 4 + xs, r.at[0]), ((1 - yh) * 4 + xs, r.at[1])]
        ins = [pltpu.make_async_copy(src, band(pc, a), s_in.at[i]) for i, (a, src) in enumerate(jobs)]
        for cp in ins:
            cp.start()
        for cp in ins:
            cp.wait()

    d = lax.dot_general(f_ref[...], pc[...], DIM0, preferred_element_type=f32)
    lo, hi = d[:U], d[U:]
    first = c == 0
    keep[step // 2, step % 2] = jnp.where(first, lo, hi)
    give[step // 2, step % 2] = jnp.where(first, hi, lo)
    for k in range(4):

        @pl.when(step == 2 * k + 1)
        def _():
            for cp in copies[k]:
                cp.start()

    @pl.when(step == 7)
    def _():
        for two in copies:
            for cp in two:
                cp.wait()


def direct(scalars, flip, own, swp, recv, *after):
    grid_spec = pltpu.PrefetchScalarGridSpec(
        num_scalar_prefetch=1,
        grid=(8,),
        in_specs=[pl.BlockSpec((8 * U, 2 * U), lambda i, s: (0, s[i]))] + [ANY] * (5 + len(after)),
        out_specs=[ANY] * 5,
        scratch_shapes=[
            pltpu.VMEM((8 * U, B), bf16),
            pltpu.VMEM((4, 2, U, B), f32),
            pltpu.VMEM((4, 2, U, B), f32),
            pltpu.SemaphoreType.DMA((8,)),
            pltpu.SemaphoreType.DMA((8,)),
        ],
    )
    out = pl.pallas_call(
        direct_kernel,
        grid_spec=grid_spec,
        out_shape=[jax.ShapeDtypeStruct((2, U, B), f32)] * 4
        + [jax.ShapeDtypeStruct((4, 2, U, B), f32)],
        compiler_params=params(),
        cost_estimate=pl.CostEstimate(flops=14_000_000_000, bytes_accessed=17_000_000, transcendentals=0),
        name="direct",
    )(scalars, flip, own, swp, *recv, *after)
    return out[:4], out[4]


def transposed_kernel(s_ref, f0, f1, *refs):
    zown, zr, pown, prr = refs[0:2], refs[2:5], refs[5], refs[6:9]
    xown, xr = refs[9:11], refs[11:14]
    refs = refs[-11:]
    outs, st_ref, pr, pc, acc, tbuf, s_in, s_out = refs[:4], *refs[4:]
    step = pl.program_id(0)
    z, yl, c = s_ref[8], s_ref[9], s_ref[10]
    copies = [pltpu.make_async_copy(tbuf.at[k], outs[k], s_out.at[k]) for k in range(4)]
    copies.append(pltpu.make_async_copy(acc, st_ref, s_out.at[4]))

    def place(zb, yb, cb):
        return (yb * 4 + zb) * 2 + cb

    rows_in = [
        (place(z, yl, c), zown[0]),
        (place(z, 1 - yl, c), zown[1]),
        (place(z, yl, 1 - c), pown.at[0]),
        (place(z, 1 - yl, 1 - c), pown.at[1]),
    ]
    for k in (1, 2, 3):
        zs = lax.rem(z + 4 - k, 4)
        for m, yb in ((0, yl), (1, 1 - yl)):
            rows_in += [(place(zs, yb, c), zr[k - 1].at[m]), (place(zs, yb, 1 - c), prr[k - 1].at[m])]
    ins = [pltpu.make_async_copy(src, band(pr, a), s_in.at[i]) for i, (a, src) in enumerate(rows_in)]
    locals_ = [xown[0], xown[1]] + [xr[3 - k].at[m] for k in (1, 2, 3) for m in (0, 1)]
    ins_c = [pltpu.make_async_copy(src, band(pc, i), s_in.at[16 + i]) for i, src in enumerate(locals_)]

    @pl.when(step == 0)
    def _():
        for cp in ins + ins_c:
            cp.start()
        acc[...] = jnp.zeros_like(acc)
        for cp in ins:
            cp.wait()

    f = jnp.concatenate([f0[...], f1[...]], axis=0)
    t = jnp.dot(f, pr[...], preferred_element_type=f32)
    tbuf[step, 0] = t[:U]
    tbuf[step, 1] = t[U:]
    for k in range(4):

        @pl.when(step == k)
        def _():
            copies[k].start()

    @pl.when(step == 0)
    def _():
        for cp in ins_c:
            cp.wait()

    hi = t.astype(bf16)
    lo = (t - hi.astype(f32)).astype(bf16)
    p = pc[pl.ds(pl.multiple_of(step * 2 * U, 2 * U), 2 * U), :]
    acc[...] += lax.dot_general(p, hi, DIM0, preferred_element_type=f32) + lax.dot_general(
        p, lo, DIM0, preferred_element_type=f32
    )

    @pl.when(step == 3)
    def _():
        copies[4].start()
        for cp in copies:
            cp.wait()


def transposed(scalars, flip, zown, zr, pown, prr, xown, xr, *after):
    grid_spec = pltpu.PrefetchScalarGridSpec(
        num_scalar_prefetch=1,
        grid=(4,),
        in_specs=[
            pl.BlockSpec((U, 16 * U), lambda i, s: (s[2 * i], 0)),
            pl.BlockSpec((U, 16 * U), lambda i, s: (s[2 * i + 1], 0)),
        ]
        + [ANY] * (14 + len(after)),
        out_specs=[ANY] * 5,
        scratch_shapes=[
            pltpu.VMEM((16 * U, B), bf16),
            pltpu.VMEM((8 * U, B), bf16),
            pltpu.VMEM((B, B), f32),
            pltpu.VMEM((4, 2, U, B), f32),
            pltpu.SemaphoreType.DMA((24,)),
            pltpu.SemaphoreType.DMA((5,)),
        ],
    )
    out = pl.pallas_call(
        transposed_kernel,
        grid_spec=grid_spec,
        out_shape=[jax.ShapeDtypeStruct((2, U, B), f32)] * 4 + [jax.ShapeDtypeStruct((B, B), f32)],
        compiler_params=params(),
        cost_estimate=pl.CostEstimate(flops=15_000_000_000, bytes_accessed=17_000_000, transcendentals=0),
        name="transposed",
    )(scalars, flip, flip, *zown, *zr, pown, *prr, *xown, *xr, *after)
    return out[:4], out[4]


def ring_kernel(a, b, c, d, *refs):
    refs[-1][...] = (a[...] + c[...]) + (b[...] + d[...])


def ring_sum(a, b, c, d, *after):
    return pl.pallas_call(
        ring_kernel,
        out_shape=jax.ShapeDtypeStruct((CH, BLK), f32),
        in_specs=[whole()] * 4 + [ANY] * len(after),
        out_specs=whole(),
        compiler_params=params(),
        cost_estimate=pl.CostEstimate(flops=100_000, bytes_accessed=500_000, transcendentals=0),
        name="ring_sum",
    )(a, b, c, d, *after)


def pack_kernel(s_ref, g_ref, st_ref, *refs):
    mine, other, flat = refs[:4], refs[4], refs[5]
    c, y = s_ref[0], s_ref[1]
    for n, (i, j) in enumerate(LOWER):
        flat[n * BLK : (n + 1) * BLK, :] = block(g_ref, i, j) - block(st_ref, i, j) - block(st_ref, j, i).T
    for k in range(4):
        q = lax.rem(y + k, 4)
        mine[k][...] = flat[pl.ds(pl.multiple_of((c * 4 + q) * CH, CH), CH), :]
        other[k] = flat[pl.ds(pl.multiple_of(((1 - c) * 4 + q) * CH, CH), CH), :]


def pack(scalars, g, st):
    out = pl.pallas_call(
        pack_kernel,
        out_shape=[jax.ShapeDtypeStruct((CH, BLK), f32)] * 4 + [jax.ShapeDtypeStruct((4, CH, BLK), f32)],
        in_specs=[pl.BlockSpec(memory_space=pltpu.SMEM)] + [whole()] * 2,
        out_specs=[whole()] * 5,
        scratch_shapes=[pltpu.VMEM((8 * CH, BLK), f32)],
        compiler_params=params(),
        cost_estimate=pl.CostEstimate(flops=2_000_000, bytes_accessed=3_000_000, transcendentals=0),
        name="pack",
    )(scalars, g, st)
    return out[:4], out[4]


def split(a):
    hi = a.astype(bf16)
    return hi, (a - hi.astype(f32)).astype(bf16)


def cat(parts, axis):
    return parts[0] if len(parts) == 1 else jnp.concatenate(parts, axis=axis)


def cat2(pairs, axis):
    return cat([p[0] for p in pairs], axis), cat([p[1] for p in pairs], axis)


def dot3(a, b):
    return jnp.dot(cat([a[0], a[0], a[1]], 1), cat([b[0], b[1], b[0]], 0), preferred_element_type=f32)


def tail_kernel(s_ref, mine, other, l_ref, inv_ref, dg_ref, *refs):
    out_ref, flat = refs[-2:]
    c, y = s_ref[0], s_ref[1]
    for k in range(4):
        q = lax.rem(y + 4 - k, 4)
        flat[pl.ds(pl.multiple_of((c * 4 + q) * CH, CH), CH), :] = mine[k]
        flat[pl.ds(pl.multiple_of(((1 - c) * 4 + q) * CH, CH), CH), :] = other[k]
    rows, cols = iotas(BLK)
    tri = rows >= cols
    low = {ij: block(l_ref, *ij) for ij in LOWER}
    for i in range(NB):
        low[i, i] = jnp.where(tri, low[i, i], 0.0)
    low_t = {ij: split(v.T) for ij, v in low.items()}
    low_n = {ij: split(v) for ij, v in low.items()}
    inv_n = [split(inv_ref[i]) for i in range(NB)]
    inv_t = [split(inv_ref[i].T) for i in range(NB)]
    q = {ij: flat[n * BLK : (n + 1) * BLK, :] for n, ij in enumerate(LOWER)}
    acc = {i: cat([q[i, j] for j in range(i + 1)], 1) for i in range(NB)}
    new = {}
    for i in reversed(range(NB)):
        con = dot3(inv_t[i], split(acc[i]))
        if i:
            part = tuple(v[:, : i * BLK] for v in split(con))
            upd = dot3(cat2([low_t[i, r] for r in range(i)], 0), part)
            for r in range(i):
                acc[r] = acc[r] - upd[r * BLK : (r + 1) * BLK, : (r + 1) * BLK]
        n = dg_ref[i * BLK : (i + 1) * BLK, : (i + 1) * BLK] - con
        corner = jnp.where(tri, n[:, i * BLK :], 0.0)
        new[i] = split(corner if i == 0 else cat([n[:, : i * BLK], corner], 1))
    keep = jnp.where(rows > cols, 1.0, jnp.where(rows == cols, 0.5, 0.0))
    inner = {}
    for i in range(NB):
        width = (i + 1) * BLK
        r = dot3(
            cat2([low_t[k, i] for k in range(i, NB)], 1),
            cat2([tuple(v[:, :width] for v in new[k]) for k in range(i, NB)], 0),
        )
        parts = [] if i == 0 else [r[:, : i * BLK]]
        parts.append(r[:, i * BLK :] * keep)
        if width < B:
            parts.append(jnp.zeros((BLK, B - width), f32))
        inner[i] = cat(parts, 1)
    left = {}
    for i in reversed(range(NB)):
        left[i] = dot3(inv_t[i], split(inner[i]))
        if i:
            upd = dot3(cat2([low_t[i, r] for r in range(i)], 0), split(left[i]))
            for r in range(i):
                inner[r] = inner[r] - upd[r * BLK : (r + 1) * BLK]
    acc = cat([left[i] for i in range(NB)], 0)
    right = {}
    for j in reversed(range(NB)):
        right[j] = dot3(split(acc[:, j * BLK : (j + 1) * BLK]), inv_n[j])
        if j:
            upd = dot3(split(right[j]), cat2([low_n[j, r] for r in range(j)], 1))
            acc = acc[:, : j * BLK] - upd
    for i in range(NB):
        for j in range(i + 1):
            v = 0.5 * (right[j][i * BLK : (i + 1) * BLK] + right[i][j * BLK : (j + 1) * BLK].T)
            out_ref[i * BLK : (i + 1) * BLK, j * BLK : (j + 1) * BLK] = v
            if i != j:
                out_ref[j * BLK : (j + 1) * BLK, i * BLK : (i + 1) * BLK] = v.T


def tail(scalars, mine, other, lower, inv, diag_grad, *after):
    return pl.pallas_call(
        tail_kernel,
        out_shape=jax.ShapeDtypeStruct((B, B), f32),
        in_specs=[pl.BlockSpec(memory_space=pltpu.SMEM)] + [whole()] * 5 + [ANY] * len(after),
        out_specs=whole(),
        scratch_shapes=[pltpu.VMEM((8 * CH, BLK), f32)],
        compiler_params=params(),
        cost_estimate=pl.CostEstimate(flops=8_000_000_000, bytes_accessed=5_000_000, transcendentals=0),
        name="tail",
    )(scalars, mine, other, lower, inv, diag_grad, *after)


def solve_kernel(r_ref, d_ref, t_ref, l_ref, inv_ref, out_ref):
    r = r_ref[...] - d_ref[...] - t_ref[...]
    xs = {}
    for j in reversed(range(NB)):
        acc = r[:, j * BLK : (j + 1) * BLK]
        for k in range(j + 1, NB):
            acc = acc - hi_dot(xs[k], block(l_ref, k, j), ((1,), (0,)))
        xs[j] = hi_dot(acc, inv_ref[j], ((1,), (0,)))
        out_ref[:, j * BLK : (j + 1) * BLK] = xs[j]


def solve(r, d, t, lower, inv):
    return pl.pallas_call(
        solve_kernel,
        out_shape=jax.ShapeDtypeStruct((U, B), f32),
        in_specs=[whole()] * 5,
        out_specs=whole(),
        compiler_params=params(),
        cost_estimate=pl.CostEstimate(flops=1_000_000_000, bytes_accessed=3_000_000, transcendentals=0),
        name="solve",
    )(r, d, t, lower, inv)


def on_device(trailing_grad, panel, panel_grad, diag_factor, diag_grad):
    flip = trailing_grad.reshape(-1, trailing_grad.shape[3])
    x, yh = lax.axis_index("x"), lax.axis_index("yh")
    z, yl, c = lax.axis_index("z"), lax.axis_index("yl"), lax.axis_index("c")
    y = yh * 2 + yl
    ints = lambda *v: jnp.stack([jnp.asarray(e, jnp.int32) for e in v])
    d_scal = ints(*[(yl ^ m) * 4 + (z + k) % 4 for k in range(4) for m in range(2)], x, yh, c)
    t_scal = ints(*[(yh ^ m) * 4 + (x + k) % 4 for k in range(4) for m in range(2)], z, yl, c, x, yh)
    cy = ints(c, y)

    x_swp = shift(panel, "yh", 1, 2)
    z_swp = shift(panel, "yl", 1, 2)
    inv, g = prep(diag_factor, panel_grad, panel)
    x_two, z_two = pair(panel, x_swp, z_swp, inv)
    x_recv = [None] * 4
    z_recv = [None] * 4
    for k in (2, 1, 3):
        z_recv[k] = shift(z_two, "z", k)
        x_recv[k] = shift(x_two, "x", k)
    pair_own = shift(z_two, "c", 1, 2)
    pair_recv = [None] + [shift(z_recv[k], "c", 1, 2) for k in (1, 2, 3)]

    d_mine, d_other = direct(d_scal, flip, panel, x_swp, x_recv[1:], *z_recv[1:])
    d_pair = shift(d_other, "c", 1, 2)
    t_own, st = transposed(
        t_scal, flip, (panel, z_swp), z_recv[1:], pair_own, pair_recv[1:], (panel, x_swp), x_recv[1:]
    )

    half = lambda v: (v * 64.0).astype(f16)
    full = lambda v: v.astype(f32) * (1 / 64.0)
    t_in = [None] * 4
    for k in (2, 1, 3):
        t_in[k] = shift(half(t_own[k]), "x", k)
    d_sum = [d_mine[k] + d_pair[k] for k in range(4)]
    d_in = [None] * 4
    for k in (2, 1, 3):
        d_in[k] = shift(half(d_sum[k]), "z", k)
    t_far = t_own[0][1] + (full(t_in[1][1]) + full(t_in[2][1]) + full(t_in[3][1]))
    d_far = d_sum[0][1] + (full(d_in[1][1]) + full(d_in[2][1]) + full(d_in[3][1]))
    t_last = shift(t_far, "yh", 1, 2)
    d_last = shift(d_far, "yl", 1, 2)
    near = (
        panel_grad
        - (t_own[0][0] + (full(t_in[1][0]) + full(t_in[2][0]) + full(t_in[3][0])))
        - (d_sum[0][0] + (full(d_in[1][0]) + full(d_in[2][0]) + full(d_in[3][0])))
    )
    panel_adj = solve(near, d_last, t_last, diag_factor, inv)

    q_mine, q_other = pack(cy, g, st)
    q_pair = shift(q_other, "c", 1, 2)
    q = [q_mine[k] + q_pair[k] for k in range(4)]
    q_in = [shift(q[k], ("yh", "yl"), k) for k in (1, 2, 3)]
    part = q[0] + q_in[0] + q_in[1] + q_in[2]
    part = ring_sum(part, *[shift(part, "z", k) for k in (1, 2, 3)])
    part = ring_sum(part, *[shift(part, "x", k) for k in (1, 2, 3)], t_far, d_far)
    q_all = jnp.stack([part] + [shift(part, ("yh", "yl"), k) for k in (1, 2, 3)])
    diag_adj = tail(cy, q_all, shift(q_all, "c", 1, 2), diag_factor, inv, diag_grad)
    return panel_adj, diag_adj


def solution(mesh):
    fine = Mesh(mesh.devices.reshape(2, 4, 2, 4, 2), ("yh", "x", "yl", "z", "c"))
    row, col = ("yh", "x"), ("yl", "z", "c")
    return jax.shard_map(
        on_device,
        mesh=fine,
        in_specs=(P(None, col, None, row), P(row + col, None), P(row + col, None), P(), P()),
        out_specs=(P(row + col, None), P()),
        check_vma=False,
    )
```

```python
import functools

import jax
import jax.numpy as jnp
from jax import lax
from jax.experimental import pallas as pl
from jax.experimental.pallas import tpu as pltpu
from jax.sharding import Mesh, PartitionSpec as P

f32 = jnp.float32
bf16 = jnp.bfloat16
f16 = jnp.float16
U = 192
B = 512
BLK = 128
NB = B // BLK
LOWER = [(i, j) for i in range(NB) for j in range(i + 1)]
CH = len(LOWER) * BLK // 8
VMEM_LIMIT = 60 * 1024 * 1024
NEAR = (1, 3, 2)


def whole():
    return pl.BlockSpec(memory_space=pltpu.VMEM)


def params(**kw):
    return pltpu.CompilerParams(vmem_limit_bytes=VMEM_LIMIT, **kw)


def hi_dot(a, b, dims):
    return lax.dot_general(
        a, b, (dims, ((), ())), precision=lax.Precision.HIGHEST, preferred_element_type=f32
    )


def shift(x, axis, k, n=4):
    return lax.ppermute(x, axis, [(i, (i + k) % n) for i in range(n)])


def after(x, *done):
    return lax.optimization_barrier((x, *done))[0]


def iotas(n):
    return (
        lax.broadcasted_iota(jnp.int32, (n, n), 0),
        lax.broadcasted_iota(jnp.int32, (n, n), 1),
    )


def block(ref, i, j):
    return ref[i * BLK : (i + 1) * BLK, j * BLK : (j + 1) * BLK]


def prep_kernel(l_ref, pg_ref, p_ref, inv_ref, g_ref):
    rows, cols = iotas(BLK)
    blocks = []
    inv = []
    for b in range(NB):
        m = jnp.where(rows >= cols, block(l_ref, b, b), 0.0)
        blocks.append(m)
        inv.append(jnp.where(rows == cols, 1.0 / jnp.where(rows == cols, m, 1.0), 0.0))
    s = 1
    while s < BLK:
        sel = (rows // s != cols // s) & (rows // (2 * s) == cols // (2 * s))
        right = [hi_dot(jnp.where(sel, blocks[b], 0.0), inv[b], ((1,), (0,))) for b in range(NB)]
        inv = [inv[b] - hi_dot(inv[b], right[b], ((1,), (0,))) for b in range(NB)]
        s *= 2
    for b in range(NB):
        inv_ref[b] = inv[b]
    p = p_ref[...]
    g = pg_ref[...]
    total = None
    for _ in range(3):
        part = g.astype(bf16)
        g = g - part.astype(f32)
        term = lax.dot_general(part, p, (((0,), (0,)), ((), ())), preferred_element_type=f32)
        total = term if total is None else total + term
    g_ref[...] = total


def prep(lower, panel_grad, panel):
    return pl.pallas_call(
        prep_kernel,
        out_shape=(
            jax.ShapeDtypeStruct((NB, BLK, BLK), f32),
            jax.ShapeDtypeStruct((B, B), f32),
        ),
        in_specs=[whole()] * 3,
        out_specs=(whole(), whole()),
        compiler_params=params(),
        cost_estimate=pl.CostEstimate(flops=4_000_000_000, bytes_accessed=3_000_000, transcendentals=0),
        name="prep",
    )(lower, panel_grad, panel)


DIM0 = (((0,), (0,)), ((), ()))
ANY = pl.BlockSpec(memory_space=pl.ANY)


def band(ref, i):
    return ref.at[pl.ds(pl.multiple_of(i * U, U), U), :]


def pair_kernel(p, xs, zs, *refs):
    x_two, z_two = refs[-2:]
    x_two[0] = p[...]
    z_two[0] = p[...]
    x_two[1] = xs[...]
    z_two[1] = zs[...]


def pair(p, xs, zs, *after):
    return pl.pallas_call(
        pair_kernel,
        out_shape=[jax.ShapeDtypeStruct((2, U, B), bf16)] * 2,
        in_specs=[whole()] * 3 + [ANY] * len(after),
        out_specs=[whole()] * 2,
        compiler_params=params(),
        cost_estimate=pl.CostEstimate(flops=0, bytes_accessed=1_600_000, transcendentals=0),
        name="pair",
    )(p, xs, zs, *after)


def direct_kernel(f_hbm, x_two, r1, r3, r2, *refs):
    mine, other, fbuf, pc, keep, give, s_f, s_in, s_out = refs[-9:]
    x, yh = lax.axis_index("x"), lax.axis_index("yh")
    z, yl, c = lax.axis_index("z"), lax.axis_index("yl"), lax.axis_index("c")

    def f_copy(i):
        k, m = i // 2, lax.rem(i, 2)
        pair_at = lax.rem(yl + m, 2) * 4 + lax.rem(z + k, 4)
        cols = pl.ds(pl.multiple_of(pair_at * 2 * U, 2 * U), 2 * U)
        return pltpu.make_async_copy(f_hbm.at[:, cols], fbuf.at[lax.rem(i, 2)], s_f.at[lax.rem(i, 2)])

    jobs = [(yh * 4 + x, x_two.at[0]), ((1 - yh) * 4 + x, x_two.at[1])]
    for k, r in zip(NEAR, (r1, r3, r2)):
        xs = lax.rem(x + 4 - k, 4)
        jobs += [(yh * 4 + xs, r.at[0]), ((1 - yh) * 4 + xs, r.at[1])]
    ins = [pltpu.make_async_copy(src, band(pc, a), s_in.at[i]) for i, (a, src) in enumerate(jobs)]
    f_copy(0).start()
    for cp in ins:
        cp.start()
    for cp in ins:
        cp.wait()

    def out_copies(k):
        return (
            pltpu.make_async_copy(keep.at[k], mine.at[k], s_out.at[k]),
            pltpu.make_async_copy(give.at[k], other.at[k], s_out.at[4 + k]),
        )

    def step(i, _):
        @pl.when(i < 7)
        def _():
            f_copy(i + 1).start()

        f_copy(i).wait()
        d = lax.dot_general(fbuf[lax.rem(i, 2)], pc[...], DIM0, preferred_element_type=f32)
        lo, hi = d[:U], d[U:]
        k, m = i // 2, lax.rem(i, 2)
        keep[k, m] = jnp.where(c == 0, lo, hi)
        give[k, m] = jnp.where(c == 0, hi, lo)

        @pl.when(m == 1)
        def _():
            for cp in out_copies(k):
                cp.start()

        return 0

    lax.fori_loop(0, 8, step, 0)
    for k in range(4):
        for cp in out_copies(k):
            cp.wait()


def direct(flip, x_two, recv, *after):
    return pl.pallas_call(
        direct_kernel,
        in_specs=[ANY] * (5 + len(after)),
        out_specs=[ANY] * 2,
        scratch_shapes=[
            pltpu.VMEM((2, 8 * U, 2 * U), bf16),
            pltpu.VMEM((8 * U, B), bf16),
            pltpu.VMEM((4, 2, U, B), f32),
            pltpu.VMEM((4, 2, U, B), f32),
            pltpu.SemaphoreType.DMA((2,)),
            pltpu.SemaphoreType.DMA((8,)),
            pltpu.SemaphoreType.DMA((8,)),
        ],
        out_shape=[jax.ShapeDtypeStruct((4, 2, U, B), f32)] * 2,
        compiler_params=params(),
        cost_estimate=pl.CostEstimate(flops=14_000_000_000, bytes_accessed=17_000_000, transcendentals=0),
        name="direct",
    )(flip, x_two, *recv, *after)


def transposed_kernel(f_hbm, z_all, p_all, x_two, r1, r3, r2, g_hbm, *refs):
    out, mine, other, fbuf, pr, pc, acc, g, tbuf, flat, s_f, s_in, s_out = refs[-13:]
    x, yh = lax.axis_index("x"), lax.axis_index("yh")
    z, yl, c = lax.axis_index("z"), lax.axis_index("yl"), lax.axis_index("c")
    y = yh * 2 + yl

    def f_copies(k):
        slot = lax.rem(k, 2)
        made = []
        for m in (0, 1):
            a = lax.rem(yh + m, 2) * 4 + lax.rem(x + k, 4)
            made.append(pltpu.make_async_copy(band(f_hbm, a), fbuf.at[slot, pl.ds(m * U, U)], s_f.at[slot, m]))
        return made

    first = []
    for k in range(4):
        zs = lax.rem(z + 4 - k, 4)
        for m, yb in ((0, yl), (1, 1 - yl)):
            first.append(((yb * 4 + zs) * 2 + c, z_all.at[k, m]))
            first.append(((yb * 4 + zs) * 2 + 1 - c, p_all.at[k, m]))
    ins = [pltpu.make_async_copy(src, band(pr, a), s_in.at[i]) for i, (a, src) in enumerate(first)]
    local_rows = {0: x_two}
    for k, r in zip(NEAR, (r1, r3, r2)):
        local_rows[4 - k] = r
    late = [
        pltpu.make_async_copy(r.at[m], band(pc, 2 * k + m), s_in.at[16 + 2 * k + m])
        for k, r in local_rows.items()
        for m in (0, 1)
    ]
    late.append(pltpu.make_async_copy(g_hbm, g, s_in.at[24]))
    for cp in f_copies(0) + ins:
        cp.start()
    acc[...] = jnp.zeros_like(acc)
    for cp in ins:
        cp.wait()
    for cp in late:
        cp.start()

    def out_copy(k):
        return pltpu.make_async_copy(tbuf.at[k], out.at[k], s_out.at[k])

    def step(k, _):
        @pl.when(k < 3)
        def _():
            for cp in f_copies(k + 1):
                cp.start()

        for cp in f_copies(k):
            cp.wait()
        t = jnp.dot(fbuf[lax.rem(k, 2)], pr[...], preferred_element_type=f32)
        tbuf[k, 0] = t[:U]
        tbuf[k, 1] = t[U:]
        out_copy(k).start()

        @pl.when(k == 0)
        def _():
            for cp in late:
                cp.wait()

        hi = t.astype(bf16)
        lo = (t - hi.astype(f32)).astype(bf16)
        p = pc[pl.ds(pl.multiple_of(k * 2 * U, 2 * U), 2 * U), :]
        acc[...] += lax.dot_general(p, hi, DIM0, preferred_element_type=f32) + lax.dot_general(
            p, lo, DIM0, preferred_element_type=f32
        )
        return 0

    lax.fori_loop(0, 4, step, 0)
    for n, (i, j) in enumerate(LOWER):
        flat[n * BLK : (n + 1) * BLK, :] = block(g, i, j) - block(acc, i, j) - block(acc, j, i).T
    for k in range(4):
        q = lax.rem(y + k, 4)
        mine[k] = flat[pl.ds(pl.multiple_of((c * 4 + q) * CH, CH), CH), :]
        other[k] = flat[pl.ds(pl.multiple_of(((1 - c) * 4 + q) * CH, CH), CH), :]
    for k in range(4):
        out_copy(k).wait()


def transposed(flip, z_all, p_all, x_two, xr, g, *after):
    return pl.pallas_call(
        transposed_kernel,
        in_specs=[ANY] * (8 + len(after)),
        out_specs=[ANY, whole(), whole()],
        scratch_shapes=[
            pltpu.VMEM((2, 2 * U, 16 * U), bf16),
            pltpu.VMEM((16 * U, B), bf16),
            pltpu.VMEM((8 * U, B), bf16),
            pltpu.VMEM((B, B), f32),
            pltpu.VMEM((B, B), f32),
            pltpu.VMEM((4, 2, U, B), f32),
            pltpu.VMEM((8 * CH, BLK), f32),
            pltpu.SemaphoreType.DMA((2, 2)),
            pltpu.SemaphoreType.DMA((25,)),
            pltpu.SemaphoreType.DMA((4,)),
        ],
        out_shape=[
            jax.ShapeDtypeStruct((4, 2, U, B), f32),
            jax.ShapeDtypeStruct((4, CH, BLK), f32),
            jax.ShapeDtypeStruct((4, CH, BLK), f32),
        ],
        compiler_params=params(),
        cost_estimate=pl.CostEstimate(flops=15_000_000_000, bytes_accessed=17_000_000, transcendentals=0),
        name="transposed",
    )(flip, z_all, p_all, x_two, *xr, g, *after)


def split(a):
    hi = a.astype(bf16)
    return hi, (a - hi.astype(f32)).astype(bf16)


def cat(parts, axis):
    return parts[0] if len(parts) == 1 else jnp.concatenate(parts, axis=axis)


def cat2(pairs, axis):
    return cat([p[0] for p in pairs], axis), cat([p[1] for p in pairs], axis)


def dot3(a, b):
    return jnp.dot(cat([a[0], a[0], a[1]], 1), cat([b[0], b[1], b[0]], 0), preferred_element_type=f32)


def tail_kernel(mine, other, l_ref, inv_ref, dg_ref, *refs):
    out_ref, flat = refs[-2:]
    c, y = lax.axis_index("c"), lax.axis_index("yh") * 2 + lax.axis_index("yl")
    for k in range(4):
        q = lax.rem(y + 4 - k, 4)
        flat[pl.ds(pl.multiple_of((c * 4 + q) * CH, CH), CH), :] = mine[k]
        flat[pl.ds(pl.multiple_of(((1 - c) * 4 + q) * CH, CH), CH), :] = other[k]
    rows, cols = iotas(BLK)
    tri = rows >= cols
    low = {ij: block(l_ref, *ij) for ij in LOWER}
    for i in range(NB):
        low[i, i] = jnp.where(tri, low[i, i], 0.0)
    low_t = {ij: split(v.T) for ij, v in low.items()}
    low_n = {ij: split(v) for ij, v in low.items()}
    inv_n = [split(inv_ref[i]) for i in range(NB)]
    inv_t = [split(inv_ref[i].T) for i in range(NB)]
    q = {ij: flat[n * BLK : (n + 1) * BLK, :] for n, ij in enumerate(LOWER)}
    acc = {i: cat([q[i, j] for j in range(i + 1)], 1) for i in range(NB)}
    new = {}
    for i in reversed(range(NB)):
        con = dot3(inv_t[i], split(acc[i]))
        if i:
            part = tuple(v[:, : i * BLK] for v in split(con))
            upd = dot3(cat2([low_t[i, r] for r in range(i)], 0), part)
            for r in range(i):
                acc[r] = acc[r] - upd[r * BLK : (r + 1) * BLK, : (r + 1) * BLK]
        n = dg_ref[i * BLK : (i + 1) * BLK, : (i + 1) * BLK] - con
        corner = jnp.where(tri, n[:, i * BLK :], 0.0)
        new[i] = split(corner if i == 0 else cat([n[:, : i * BLK], corner], 1))
    keep = jnp.where(rows > cols, 1.0, jnp.where(rows == cols, 0.5, 0.0))
    inner = {}
    for i in range(NB):
        width = (i + 1) * BLK
        r = dot3(
            cat2([low_t[k, i] for k in range(i, NB)], 1),
            cat2([tuple(v[:, :width] for v in new[k]) for k in range(i, NB)], 0),
        )
        parts = [] if i == 0 else [r[:, : i * BLK]]
        parts.append(r[:, i * BLK :] * keep)
        if width < B:
            parts.append(jnp.zeros((BLK, B - width), f32))
        inner[i] = cat(parts, 1)
    left = {}
    for i in reversed(range(NB)):
        left[i] = dot3(inv_t[i], split(inner[i]))
        if i:
            upd = dot3(cat2([low_t[i, r] for r in range(i)], 0), split(left[i]))
            for r in range(i):
                inner[r] = inner[r] - upd[r * BLK : (r + 1) * BLK]
    acc = cat([left[i] for i in range(NB)], 0)
    right = {}
    for j in reversed(range(NB)):
        right[j] = dot3(split(acc[:, j * BLK : (j + 1) * BLK]), inv_n[j])
        if j:
            upd = dot3(split(right[j]), cat2([low_n[j, r] for r in range(j)], 1))
            acc = acc[:, : j * BLK] - upd
    for i in range(NB):
        for j in range(i + 1):
            v = 0.5 * (right[j][i * BLK : (i + 1) * BLK] + right[i][j * BLK : (j + 1) * BLK].T)
            out_ref[i * BLK : (i + 1) * BLK, j * BLK : (j + 1) * BLK] = v
            if i != j:
                out_ref[j * BLK : (j + 1) * BLK, i * BLK : (i + 1) * BLK] = v.T


def tail(mine, other, lower, inv, diag_grad, *after):
    return pl.pallas_call(
        tail_kernel,
        out_shape=jax.ShapeDtypeStruct((B, B), f32),
        in_specs=[whole()] * 5 + [ANY] * len(after),
        out_specs=whole(),
        scratch_shapes=[pltpu.VMEM((8 * CH, BLK), f32)],
        compiler_params=params(),
        cost_estimate=pl.CostEstimate(flops=8_000_000_000, bytes_accessed=5_000_000, transcendentals=0),
        name="tail",
    )(mine, other, lower, inv, diag_grad, *after)


def solve_kernel(r_ref, d_ref, t_ref, l_ref, inv_ref, out_ref):
    acc = r_ref[...] - d_ref[...] - t_ref[...]
    for j in reversed(range(NB)):
        x = dot3(split(acc[:, j * BLK :]), split(inv_ref[j]))
        out_ref[:, j * BLK : (j + 1) * BLK] = x
        if j:
            acc = acc[:, : j * BLK] - dot3(split(x), split(l_ref[j * BLK : (j + 1) * BLK, : j * BLK]))


def solve(r, d, t, lower, inv):
    return pl.pallas_call(
        solve_kernel,
        out_shape=jax.ShapeDtypeStruct((U, B), f32),
        in_specs=[whole()] * 5,
        out_specs=whole(),
        compiler_params=params(),
        cost_estimate=pl.CostEstimate(flops=1_000_000_000, bytes_accessed=3_000_000, transcendentals=0),
        name="solve",
    )(r, d, t, lower, inv)


def on_device(trailing_grad, panel, panel_grad, diag_factor, diag_grad):
    flip = trailing_grad.reshape(-1, trailing_grad.shape[3])

    x_swp = shift(panel, "yh", 1, 2)
    z_swp = shift(panel, "yl", 1, 2)
    inv, g = prep(diag_factor, panel_grad, panel)
    x_two, z_two = pair(panel, x_swp, z_swp, inv)
    z_recv = [shift(z_two, "z", k) for k in NEAR]
    x_recv = [shift(x_two, "x", k) for k in NEAR]
    z_recv, x_recv = lax.optimization_barrier((z_recv, x_recv))
    z_all = jnp.stack([z_two, z_recv[0], z_recv[2], z_recv[1]])
    p_all = shift(z_all, "c", 1, 2)

    half = lambda v: (v * 64.0).astype(f16)
    full = lambda v: v.astype(f32) * (1 / 64.0)

    t_all, q_mine, q_other = transposed(flip, z_all, p_all, x_two, x_recv, g)
    t_in = {k: shift(half(t_all[k]), "x", k) for k in NEAR}
    q_pair = shift(q_other, "c", 1, 2)
    q = [q_mine[k] + q_pair[k] for k in range(4)]
    q_in = [shift(q[k], ("yh", "yl"), k) for k in NEAR]
    part = q[0] + q_in[0] + q_in[1] + q_in[2]
    t_far = t_all[0][1] + (full(t_in[2][1]) + full(t_in[3][1]) + full(t_in[1][1]))
    t_last = shift(t_far, "yh", 1, 2)
    x_two = after(x_two, part, t_in[1], t_in[3])
    d_mine, d_other = direct(flip, x_two, x_recv)
    d_pair = shift(d_other, "c", 1, 2)
    got = {k: shift(part, "z", k) for k in NEAR}
    part = (part + got[2]) + (got[1] + got[3])
    d_pair = after(d_pair, part)
    d_own = d_mine[0] + d_pair[0]
    d_out = {k: half(d_mine[k] + d_pair[k]) for k in NEAR}
    d_in = {k: shift(d_out[k], "z", k) for k in NEAR}
    part = after(part, *d_out.values())
    got = {k: shift(part, "x", k) for k in NEAR}
    part = after(part, d_in[1], d_in[3])
    part = (part + got[2]) + (got[1] + got[3])
    q_all = jnp.stack([part] + [shift(part, ("yh", "yl"), k) for k in (1, 2, 3)])
    q_all = after(q_all, t_last)
    d_far = d_own[1] + (full(d_in[2][1]) + full(d_in[3][1]) + full(d_in[1][1]))
    d_last = shift(d_far, "yl", 1, 2)
    near = (
        panel_grad
        - (t_all[0][0] + (full(t_in[2][0]) + full(t_in[3][0]) + full(t_in[1][0])))
        - (d_own[0] + (full(d_in[2][0]) + full(d_in[3][0]) + full(d_in[1][0])))
    )
    q_pair = after(shift(q_all, "c", 1, 2), d_far)
    diag_adj = tail(q_all, q_pair, diag_factor, inv, diag_grad)
    near = after(near, diag_adj)
    return solve(near, d_last, t_last, diag_factor, inv), diag_adj


def solution(mesh):
    fine = Mesh(mesh.devices.reshape(2, 4, 2, 4, 2), ("yh", "x", "yl", "z", "c"))
    row, col = ("yh", "x"), ("yl", "z", "c")
    return jax.shard_map(
        on_device,
        mesh=fine,
        in_specs=(P(None, col, None, row), P(row + col, None), P(row + col, None), P(), P()),
        out_specs=(P(row + col, None), P()),
        check_vma=False,
    )
```

```python
import functools

import jax
import jax.numpy as jnp
from jax import lax
from jax.experimental import pallas as pl
from jax.experimental.pallas import tpu as pltpu
from jax.sharding import Mesh, PartitionSpec as P

f32 = jnp.float32
bf16 = jnp.bfloat16
f16 = jnp.float16
U = 192
B = 512
BLK = 128
NB = B // BLK
LOWER = [(i, j) for i in range(NB) for j in range(i + 1)]
CH = len(LOWER) * BLK // 8
VMEM_LIMIT = 60 * 1024 * 1024
NEAR = (2, 3, 1)


def whole():
    return pl.BlockSpec(memory_space=pltpu.VMEM)


def params(**kw):
    return pltpu.CompilerParams(vmem_limit_bytes=VMEM_LIMIT, **kw)


def hi_dot(a, b, dims):
    return lax.dot_general(
        a, b, (dims, ((), ())), precision=lax.Precision.HIGHEST, preferred_element_type=f32
    )


def shift(x, axis, k, n=4):
    return lax.ppermute(x, axis, [(i, (i + k) % n) for i in range(n)])


def after(x, *done):
    return lax.optimization_barrier((x, *done))[0]


def swap(x, axis, far):
    return lax.ppermute(x, axis, [(i, 3 - i if far else i ^ 1) for i in range(4)])


def chunk_order(y):
    near = y + 1 - 2 * lax.rem(y, 2)
    return (y, 3 - y, near, 3 - near)


def iotas(n):
    return (
        lax.broadcasted_iota(jnp.int32, (n, n), 0),
        lax.broadcasted_iota(jnp.int32, (n, n), 1),
    )


def block(ref, i, j):
    return ref[i * BLK : (i + 1) * BLK, j * BLK : (j + 1) * BLK]


def prep_kernel(l_ref, pg_ref, p_ref, inv_ref, g_ref):
    rows, cols = iotas(BLK)
    blocks = []
    inv = []
    for b in range(NB):
        m = jnp.where(rows >= cols, block(l_ref, b, b), 0.0)
        blocks.append(m)
        inv.append(jnp.where(rows == cols, 1.0 / jnp.where(rows == cols, m, 1.0), 0.0))
    s = 1
    while s < BLK:
        sel = (rows // s != cols // s) & (rows // (2 * s) == cols // (2 * s))
        right = [hi_dot(jnp.where(sel, blocks[b], 0.0), inv[b], ((1,), (0,))) for b in range(NB)]
        inv = [inv[b] - hi_dot(inv[b], right[b], ((1,), (0,))) for b in range(NB)]
        s *= 2
    for b in range(NB):
        inv_ref[b] = inv[b]
    p = p_ref[...]
    g = pg_ref[...]
    total = None
    for _ in range(3):
        part = g.astype(bf16)
        g = g - part.astype(f32)
        term = lax.dot_general(part, p, (((0,), (0,)), ((), ())), preferred_element_type=f32)
        total = term if total is None else total + term
    g_ref[...] = total


def prep(lower, panel_grad, panel):
    return pl.pallas_call(
        prep_kernel,
        out_shape=(
            jax.ShapeDtypeStruct((NB, BLK, BLK), f32),
            jax.ShapeDtypeStruct((B, B), f32),
        ),
        in_specs=[whole()] * 3,
        out_specs=(whole(), whole()),
        compiler_params=params(),
        cost_estimate=pl.CostEstimate(flops=4_000_000_000, bytes_accessed=3_000_000, transcendentals=0),
        name="prep",
    )(lower, panel_grad, panel)


DIM0 = (((0,), (0,)), ((), ()))
ANY = pl.BlockSpec(memory_space=pl.ANY)


def band(ref, i):
    return ref.at[pl.ds(pl.multiple_of(i * U, U), U), :]


def direct_kernel(f_hbm, x_two, r2, r3, r1, *refs):
    mine, other, fbuf, pc, keep, give, s_f, s_in, s_out = refs[-9:]
    x, yh = lax.axis_index("x"), lax.axis_index("yh")
    z, yl, c = lax.axis_index("z"), lax.axis_index("yl"), lax.axis_index("c")

    def f_copies(k):
        slot = lax.rem(k, 2)
        made = []
        for m in (0, 1):
            at = lax.rem(yl + m, 2) * 4 + lax.rem(z + k, 4)
            cols = pl.ds(pl.multiple_of(at * 2 * U, 2 * U), 2 * U)
            dst = fbuf.at[slot, :, m * 2 * U : (m + 1) * 2 * U]
            made.append(pltpu.make_async_copy(f_hbm.at[:, cols], dst, s_f.at[slot, m]))
        return made

    jobs = [(yh * 4 + x, x_two.at[0]), ((1 - yh) * 4 + x, x_two.at[1])]
    for k, r in zip(NEAR, (r2, r3, r1)):
        xs = lax.rem(x + 4 - k, 4)
        jobs += [(yh * 4 + xs, r.at[0]), ((1 - yh) * 4 + xs, r.at[1])]
    ins = [pltpu.make_async_copy(src, band(pc, a), s_in.at[i]) for i, (a, src) in enumerate(jobs)]
    for cp in f_copies(0) + ins:
        cp.start()
    for cp in ins:
        cp.wait()

    def out_copies(k):
        return (
            pltpu.make_async_copy(keep.at[k], mine.at[k], s_out.at[k]),
            pltpu.make_async_copy(give.at[k], other.at[k], s_out.at[4 + k]),
        )

    def step(k, _):
        @pl.when(k < 3)
        def _():
            for cp in f_copies(k + 1):
                cp.start()

        for cp in f_copies(k):
            cp.wait()
        d = lax.dot_general(fbuf[lax.rem(k, 2)], pc[...], DIM0, preferred_element_type=f32)
        for m in (0, 1):
            lo, hi = d[2 * m * U : (2 * m + 1) * U], d[(2 * m + 1) * U : (2 * m + 2) * U]
            keep[k, m] = jnp.where(c == 0, lo, hi)
            give[k, m] = jnp.where(c == 0, hi, lo)
        for cp in out_copies(k):
            cp.start()
        return 0

    lax.fori_loop(0, 4, step, 0)
    for k in range(4):
        for cp in out_copies(k):
            cp.wait()


def direct(flip, x_two, recv, *after):
    return pl.pallas_call(
        direct_kernel,
        in_specs=[ANY] * (5 + len(after)),
        out_specs=[ANY] * 2,
        scratch_shapes=[
            pltpu.VMEM((2, 8 * U, 4 * U), bf16),
            pltpu.VMEM((8 * U, B), bf16),
            pltpu.VMEM((4, 2, U, B), f32),
            pltpu.VMEM((4, 2, U, B), f32),
            pltpu.SemaphoreType.DMA((2, 2)),
            pltpu.SemaphoreType.DMA((8,)),
            pltpu.SemaphoreType.DMA((8,)),
        ],
        out_shape=[jax.ShapeDtypeStruct((4, 2, U, B), f32)] * 2,
        compiler_params=params(),
        cost_estimate=pl.CostEstimate(flops=14_000_000_000, bytes_accessed=17_000_000, transcendentals=0),
        name="direct",
    )(flip, x_two, *recv, *after)


def transposed_kernel(f_hbm, z_all, p_all, x_two, r2, r3, r1, g_hbm, *refs):
    out, mine, other, fbuf, pr, pc, acc, g, tbuf, flat, s_f, s_in, s_out = refs[-13:]
    x, yh = lax.axis_index("x"), lax.axis_index("yh")
    z, yl, c = lax.axis_index("z"), lax.axis_index("yl"), lax.axis_index("c")
    y = yh * 2 + yl

    def f_copies(s):
        made = []
        for j in range(4):
            a = lax.rem(yh + j % 2, 2) * 4 + lax.rem(x + 2 * s + j // 2, 4)
            made.append(pltpu.make_async_copy(band(f_hbm, a), fbuf.at[s, pl.ds(j * U, U)], s_f.at[s, j]))
        return made

    first = []
    for k in range(4):
        zs = lax.rem(z + 4 - k, 4)
        for m, yb in ((0, yl), (1, 1 - yl)):
            first.append(((yb * 4 + zs) * 2 + c, z_all.at[k, m]))
            first.append(((yb * 4 + zs) * 2 + 1 - c, p_all.at[k, m]))
    ins = [pltpu.make_async_copy(src, band(pr, a), s_in.at[i]) for i, (a, src) in enumerate(first)]
    local_rows = {0: x_two}
    for k, r in zip(NEAR, (r2, r3, r1)):
        local_rows[4 - k] = r
    late = [
        pltpu.make_async_copy(r.at[m], band(pc, 2 * k + m), s_in.at[16 + 2 * k + m])
        for k, r in local_rows.items()
        for m in (0, 1)
    ]
    late.append(pltpu.make_async_copy(g_hbm, g, s_in.at[24]))
    for cp in f_copies(0) + ins:
        cp.start()
    acc[...] = jnp.zeros_like(acc)
    for cp in ins:
        cp.wait()
    for cp in late:
        cp.start()

    def out_copy(k):
        return pltpu.make_async_copy(tbuf.at[k], out.at[k], s_out.at[k])

    def step(s, _):
        @pl.when(s == 0)
        def _():
            for cp in f_copies(1):
                cp.start()

        for cp in f_copies(s):
            cp.wait()
        t = jnp.dot(fbuf[s], pr[...], preferred_element_type=f32)
        for j in range(4):
            tbuf[2 * s + j // 2, j % 2] = t[j * U : (j + 1) * U]
        out_copy(2 * s).start()
        out_copy(2 * s + 1).start()

        @pl.when(s == 0)
        def _():
            for cp in late:
                cp.wait()

        hi = t.astype(bf16)
        lo = (t - hi.astype(f32)).astype(bf16)
        p = pc[pl.ds(pl.multiple_of(s * 4 * U, 4 * U), 4 * U), :]
        acc[...] += lax.dot_general(p, hi, DIM0, preferred_element_type=f32) + lax.dot_general(
            p, lo, DIM0, preferred_element_type=f32
        )
        return 0

    lax.fori_loop(0, 2, step, 0)
    for n, (i, j) in enumerate(LOWER):
        flat[n * BLK : (n + 1) * BLK, :] = block(g, i, j) - block(acc, i, j) - block(acc, j, i).T
    for k, q in enumerate(chunk_order(y)):
        mine[k] = flat[pl.ds(pl.multiple_of((c * 4 + q) * CH, CH), CH), :]
        other[k] = flat[pl.ds(pl.multiple_of(((1 - c) * 4 + q) * CH, CH), CH), :]
    for k in range(4):
        out_copy(k).wait()


def transposed(flip, z_all, p_all, x_two, xr, g, *after):
    return pl.pallas_call(
        transposed_kernel,
        in_specs=[ANY] * (8 + len(after)),
        out_specs=[ANY, whole(), whole()],
        scratch_shapes=[
            pltpu.VMEM((2, 4 * U, 16 * U), bf16),
            pltpu.VMEM((16 * U, B), bf16),
            pltpu.VMEM((8 * U, B), bf16),
            pltpu.VMEM((B, B), f32),
            pltpu.VMEM((B, B), f32),
            pltpu.VMEM((4, 2, U, B), f32),
            pltpu.VMEM((8 * CH, BLK), f32),
            pltpu.SemaphoreType.DMA((2, 4)),
            pltpu.SemaphoreType.DMA((25,)),
            pltpu.SemaphoreType.DMA((4,)),
        ],
        out_shape=[
            jax.ShapeDtypeStruct((4, 2, U, B), f32),
            jax.ShapeDtypeStruct((4, CH, BLK), f32),
            jax.ShapeDtypeStruct((4, CH, BLK), f32),
        ],
        compiler_params=params(),
        cost_estimate=pl.CostEstimate(flops=15_000_000_000, bytes_accessed=17_000_000, transcendentals=0),
        name="transposed",
    )(flip, z_all, p_all, x_two, *xr, g, *after)


def split(a):
    hi = a.astype(bf16)
    return hi, (a - hi.astype(f32)).astype(bf16)


def cat(parts, axis):
    return parts[0] if len(parts) == 1 else jnp.concatenate(parts, axis=axis)


def cat2(pairs, axis):
    return cat([p[0] for p in pairs], axis), cat([p[1] for p in pairs], axis)


def dot3(a, b):
    return jnp.dot(cat([a[0], a[0], a[1]], 1), cat([b[0], b[1], b[0]], 0), preferred_element_type=f32)


def tail_kernel(mine, other, l_ref, inv_ref, dg_ref, *refs):
    out_ref, flat = refs[-2:]
    c, y = lax.axis_index("c"), lax.axis_index("yh") * 2 + lax.axis_index("yl")
    for k, q in enumerate(chunk_order(y)):
        flat[pl.ds(pl.multiple_of((c * 4 + q) * CH, CH), CH), :] = mine[k]
        flat[pl.ds(pl.multiple_of(((1 - c) * 4 + q) * CH, CH), CH), :] = other[k]
    rows, cols = iotas(BLK)
    tri = rows >= cols
    low = {ij: block(l_ref, *ij) for ij in LOWER}
    for i in range(NB):
        low[i, i] = jnp.where(tri, low[i, i], 0.0)
    low_t = {ij: split(v.T) for ij, v in low.items()}
    low_n = {ij: split(v) for ij, v in low.items()}
    inv_n = [split(inv_ref[i]) for i in range(NB)]
    inv_t = [split(inv_ref[i].T) for i in range(NB)]
    q = {ij: flat[n * BLK : (n + 1) * BLK, :] for n, ij in enumerate(LOWER)}
    acc = {i: cat([q[i, j] for j in range(i + 1)], 1) for i in range(NB)}
    new = {}
    for i in reversed(range(NB)):
        con = dot3(inv_t[i], split(acc[i]))
        if i:
            part = tuple(v[:, : i * BLK] for v in split(con))
            upd = dot3(cat2([low_t[i, r] for r in range(i)], 0), part)
            for r in range(i):
                acc[r] = acc[r] - upd[r * BLK : (r + 1) * BLK, : (r + 1) * BLK]
        n = dg_ref[i * BLK : (i + 1) * BLK, : (i + 1) * BLK] - con
        corner = jnp.where(tri, n[:, i * BLK :], 0.0)
        new[i] = split(corner if i == 0 else cat([n[:, : i * BLK], corner], 1))
    keep = jnp.where(rows > cols, 1.0, jnp.where(rows == cols, 0.5, 0.0))
    inner = {}
    for i in range(NB):
        width = (i + 1) * BLK
        r = dot3(
            cat2([low_t[k, i] for k in range(i, NB)], 1),
            cat2([tuple(v[:, :width] for v in new[k]) for k in range(i, NB)], 0),
        )
        parts = [] if i == 0 else [r[:, : i * BLK]]
        parts.append(r[:, i * BLK :] * keep)
        if width < B:
            parts.append(jnp.zeros((BLK, B - width), f32))
        inner[i] = cat(parts, 1)
    left = {}
    for i in reversed(range(NB)):
        left[i] = dot3(inv_t[i], split(inner[i]))
        if i:
            upd = dot3(cat2([low_t[i, r] for r in range(i)], 0), split(left[i]))
            for r in range(i):
                inner[r] = inner[r] - upd[r * BLK : (r + 1) * BLK]
    acc = cat([left[i] for i in range(NB)], 0)
    right = {}
    for j in reversed(range(NB)):
        right[j] = dot3(split(acc[:, j * BLK : (j + 1) * BLK]), inv_n[j])
        if j:
            upd = dot3(split(right[j]), cat2([low_n[j, r] for r in range(j)], 1))
            acc = acc[:, : j * BLK] - upd
    for i in range(NB):
        for j in range(i + 1):
            v = 0.5 * (right[j][i * BLK : (i + 1) * BLK] + right[i][j * BLK : (j + 1) * BLK].T)
            out_ref[i * BLK : (i + 1) * BLK, j * BLK : (j + 1) * BLK] = v
            if i != j:
                out_ref[j * BLK : (j + 1) * BLK, i * BLK : (i + 1) * BLK] = v.T


def tail(mine, other, lower, inv, diag_grad, *after):
    return pl.pallas_call(
        tail_kernel,
        out_shape=jax.ShapeDtypeStruct((B, B), f32),
        in_specs=[whole()] * 5 + [ANY] * len(after),
        out_specs=whole(),
        scratch_shapes=[pltpu.VMEM((8 * CH, BLK), f32)],
        compiler_params=params(),
        cost_estimate=pl.CostEstimate(flops=8_000_000_000, bytes_accessed=5_000_000, transcendentals=0),
        name="tail",
    )(mine, other, lower, inv, diag_grad, *after)


def solve_kernel(r_ref, d_ref, t_ref, l_ref, inv_ref, out_ref):
    acc = r_ref[...] - d_ref[...] - t_ref[...]
    for j in reversed(range(NB)):
        x = dot3(split(acc[:, j * BLK :]), split(inv_ref[j]))
        out_ref[:, j * BLK : (j + 1) * BLK] = x
        if j:
            acc = acc[:, : j * BLK] - dot3(split(x), split(l_ref[j * BLK : (j + 1) * BLK, : j * BLK]))


def solve(r, d, t, lower, inv):
    return pl.pallas_call(
        solve_kernel,
        out_shape=jax.ShapeDtypeStruct((U, B), f32),
        in_specs=[whole()] * 5,
        out_specs=whole(),
        compiler_params=params(),
        cost_estimate=pl.CostEstimate(flops=1_000_000_000, bytes_accessed=3_000_000, transcendentals=0),
        name="solve",
    )(r, d, t, lower, inv)


def on_device(trailing_grad, panel, panel_grad, diag_factor, diag_grad):
    flip = trailing_grad.reshape(-1, trailing_grad.shape[3])

    x_swp = shift(panel, "yh", 1, 2)
    z_swp = shift(panel, "yl", 1, 2)
    inv, g = prep(diag_factor, panel_grad, panel)
    x_swp, z_swp = after(x_swp, inv), after(z_swp, inv)
    x_two, z_two = jnp.stack([panel, x_swp]), jnp.stack([panel, z_swp])
    z_recv = [shift(z_two, "z", k) for k in NEAR]
    x_recv = [shift(x_two, "x", k) for k in NEAR]
    z_recv, x_recv = lax.optimization_barrier((z_recv, x_recv))
    z_all = jnp.stack([z_two, z_recv[2], z_recv[0], z_recv[1]])
    p_all = shift(z_all, "c", 1, 2)

    half = lambda v: (v * 64.0).astype(f16)
    full = lambda v: v.astype(f32) * (1 / 64.0)

    t_all, q_mine, q_other = transposed(flip, z_all, p_all, x_two, x_recv, g)
    t_out = {k: half(t_all[k]) for k in NEAR}
    t_in = {k: shift(t_out[k], "x", k) for k in NEAR}
    q_pair = shift(after(q_other, *t_out.values()), "c", 1, 2)
    y_axis = ("yh", "yl")
    two = q_mine[:2] + q_pair[:2] + swap(q_mine[2:] + q_pair[2:], y_axis, False)
    part = two[0] + swap(two[1], y_axis, True)
    t_sum = after(t_all[0] + (full(t_in[2]) + full(t_in[3]) + full(t_in[1])))
    t_last = shift(t_sum[1], "yh", 1, 2)
    x_two = after(x_two, part, t_in[1], t_in[3])
    d_mine, d_other = direct(flip, x_two, x_recv)
    d_pair = shift(d_other, "c", 1, 2)
    for far in (False, True):
        part = part + swap(part, "z", far)
    d_pair = after(d_pair, part)
    d_own = d_mine[0] + d_pair[0]
    d_out = {k: half(d_mine[k] + d_pair[k]) for k in NEAR}
    d_in = {k: shift(d_out[k], "z", k) for k in NEAR}
    part = after(part, *d_out.values())
    part = after(part + swap(part, "x", False), t_sum)
    part = part + swap(part, "x", True)
    part = after(part, d_in[1], d_in[3])
    two = after(jnp.stack([part, swap(part, y_axis, True)]), t_last)
    q_all = jnp.concatenate([two, swap(two, y_axis, False)])
    d_far = d_own[1] + (full(d_in[2][1]) + full(d_in[3][1]) + full(d_in[1][1]))
    d_last = shift(d_far, "yl", 1, 2)
    near = (
        panel_grad
        - t_sum[0]
        - (d_own[0] + (full(d_in[2][0]) + full(d_in[3][0]) + full(d_in[1][0])))
    )
    q_pair = after(shift(q_all, "c", 1, 2), d_far)
    diag_adj = tail(q_all, q_pair, diag_factor, inv, diag_grad)
    near = after(near, diag_adj)
    return solve(near, d_last, t_last, diag_factor, inv), diag_adj


def solution(mesh):
    fine = Mesh(mesh.devices.reshape(2, 4, 2, 4, 2), ("yh", "x", "yl", "z", "c"))
    row, col = ("yh", "x"), ("yl", "z", "c")
    return jax.shard_map(
        on_device,
        mesh=fine,
        in_specs=(P(None, col, None, row), P(row + col, None), P(row + col, None), P(), P()),
        out_specs=(P(row + col, None), P()),
        check_vma=False,
    )
```

```python
import functools

import jax
import jax.numpy as jnp
from jax import lax
from jax.experimental import pallas as pl
from jax.experimental.pallas import tpu as pltpu
from jax.sharding import Mesh, PartitionSpec as P

f32 = jnp.float32
bf16 = jnp.bfloat16
f16 = jnp.float16
U = 192
B = 512
BLK = 128
NB = B // BLK
LOWER = [(i, j) for i in range(NB) for j in range(i + 1)]
CH = len(LOWER) * BLK // 8
VMEM_LIMIT = 60 * 1024 * 1024
NEAR = (2, 3, 1)


def whole():
    return pl.BlockSpec(memory_space=pltpu.VMEM)


def params(**kw):
    return pltpu.CompilerParams(vmem_limit_bytes=VMEM_LIMIT, **kw)


def hi_dot(a, b, dims):
    return lax.dot_general(
        a, b, (dims, ((), ())), precision=lax.Precision.HIGHEST, preferred_element_type=f32
    )


def shift(x, axis, k, n=4):
    return lax.ppermute(x, axis, [(i, (i + k) % n) for i in range(n)])


def after(x, *done):
    return lax.optimization_barrier((x, *done))[0]


def swap(x, axis, far):
    return lax.ppermute(x, axis, [(i, 3 - i if far else i ^ 1) for i in range(4)])


def chunk_order(y):
    near = y + 1 - 2 * lax.rem(y, 2)
    return (y, 3 - y, near, 3 - near)


def iotas(n):
    return (
        lax.broadcasted_iota(jnp.int32, (n, n), 0),
        lax.broadcasted_iota(jnp.int32, (n, n), 1),
    )


def block(ref, i, j):
    return ref[i * BLK : (i + 1) * BLK, j * BLK : (j + 1) * BLK]


def split(a):
    hi = a.astype(bf16)
    return hi, (a - hi.astype(f32)).astype(bf16)


def prep_kernel(l_ref, pg_ref, p_ref, step_n, step_t, low_t, g_ref):
    rows, cols = iotas(BLK)
    blocks = []
    inv = []
    for b in range(NB):
        m = jnp.where(rows >= cols, block(l_ref, b, b), 0.0)
        blocks.append(m)
        inv.append(jnp.where(rows == cols, 1.0 / jnp.where(rows == cols, m, 1.0), 0.0))
    s = 1
    while s < BLK:
        sel = (rows // s != cols // s) & (rows // (2 * s) == cols // (2 * s))
        right = [hi_dot(jnp.where(sel, blocks[b], 0.0), inv[b], ((1,), (0,))) for b in range(NB)]
        inv = [inv[b] - hi_dot(inv[b], right[b], ((1,), (0,))) for b in range(NB)]
        s *= 2
    for i, j in LOWER:
        m = blocks[i] if i == j else block(l_ref, i, j)
        v = inv[i] if i == j else hi_dot(inv[i], m, ((1,), (0,)))
        at_i, at_j = slice(i * BLK, (i + 1) * BLK), slice(j * BLK, (j + 1) * BLK)
        step_n[0, at_i, at_j], step_n[1, at_i, at_j] = split(v)
        step_t[0, at_j, at_i], step_t[1, at_j, at_i] = split(v.T)
        low_t[0, at_j, at_i], low_t[1, at_j, at_i] = split(m.T)
    p = p_ref[...]
    g = pg_ref[...]
    total = None
    for _ in range(3):
        part = g.astype(bf16)
        g = g - part.astype(f32)
        term = lax.dot_general(part, p, (((0,), (0,)), ((), ())), preferred_element_type=f32)
        total = term if total is None else total + term
    g_ref[...] = total


def prep(lower, panel_grad, panel):
    return pl.pallas_call(
        prep_kernel,
        out_shape=(
            jax.ShapeDtypeStruct((2, B, B), bf16),
            jax.ShapeDtypeStruct((2, B, B), bf16),
            jax.ShapeDtypeStruct((2, B, B), bf16),
            jax.ShapeDtypeStruct((B, B), f32),
        ),
        in_specs=[whole()] * 3,
        out_specs=(whole(),) * 4,
        compiler_params=params(),
        cost_estimate=pl.CostEstimate(flops=4_000_000_000, bytes_accessed=3_000_000, transcendentals=0),
        name="prep",
    )(lower, panel_grad, panel)


DIM0 = (((0,), (0,)), ((), ()))
ANY = pl.BlockSpec(memory_space=pl.ANY)


def band(ref, i):
    return ref.at[pl.ds(pl.multiple_of(i * U, U), U), :]


def direct_kernel(f_hbm, x_two, r2, r3, r1, *refs):
    mine, other, fbuf, pc, keep, give, s_f, s_in, s_out = refs[-9:]
    x, yh = lax.axis_index("x"), lax.axis_index("yh")
    z, yl, c = lax.axis_index("z"), lax.axis_index("yl"), lax.axis_index("c")

    def f_copies(k):
        slot = lax.rem(k, 2)
        made = []
        for m in (0, 1):
            at = lax.rem(yl + m, 2) * 4 + lax.rem(z + k, 4)
            cols = pl.ds(pl.multiple_of(at * 2 * U, 2 * U), 2 * U)
            dst = fbuf.at[slot, :, m * 2 * U : (m + 1) * 2 * U]
            made.append(pltpu.make_async_copy(f_hbm.at[:, cols], dst, s_f.at[slot, m]))
        return made

    jobs = [(yh * 4 + x, x_two.at[0]), ((1 - yh) * 4 + x, x_two.at[1])]
    for k, r in zip(NEAR, (r2, r3, r1)):
        xs = lax.rem(x + 4 - k, 4)
        jobs += [(yh * 4 + xs, r.at[0]), ((1 - yh) * 4 + xs, r.at[1])]
    ins = [pltpu.make_async_copy(src, band(pc, a), s_in.at[i]) for i, (a, src) in enumerate(jobs)]
    for cp in f_copies(0) + ins:
        cp.start()
    for cp in ins:
        cp.wait()

    def out_copies(k):
        return (
            pltpu.make_async_copy(keep.at[k], mine.at[k], s_out.at[k]),
            pltpu.make_async_copy(give.at[k], other.at[k], s_out.at[4 + k]),
        )

    def step(k, _):
        @pl.when(k < 3)
        def _():
            for cp in f_copies(k + 1):
                cp.start()

        for cp in f_copies(k):
            cp.wait()
        d = lax.dot_general(fbuf[lax.rem(k, 2)], pc[...], DIM0, preferred_element_type=f32)
        for m in (0, 1):
            lo, hi = d[2 * m * U : (2 * m + 1) * U], d[(2 * m + 1) * U : (2 * m + 2) * U]
            keep[k, m] = jnp.where(c == 0, lo, hi)
            give[k, m] = jnp.where(c == 0, hi, lo)
        for cp in out_copies(k):
            cp.start()
        return 0

    lax.fori_loop(0, 4, step, 0)
    for k in range(4):
        for cp in out_copies(k):
            cp.wait()


def direct(flip, x_two, recv, *after):
    return pl.pallas_call(
        direct_kernel,
        in_specs=[ANY] * (5 + len(after)),
        out_specs=[ANY] * 2,
        scratch_shapes=[
            pltpu.VMEM((2, 8 * U, 4 * U), bf16),
            pltpu.VMEM((8 * U, B), bf16),
            pltpu.VMEM((4, 2, U, B), f32),
            pltpu.VMEM((4, 2, U, B), f32),
            pltpu.SemaphoreType.DMA((2, 2)),
            pltpu.SemaphoreType.DMA((8,)),
            pltpu.SemaphoreType.DMA((8,)),
        ],
        out_shape=[jax.ShapeDtypeStruct((4, 2, U, B), f32)] * 2,
        compiler_params=params(),
        cost_estimate=pl.CostEstimate(flops=14_000_000_000, bytes_accessed=17_000_000, transcendentals=0),
        name="direct",
    )(flip, x_two, *recv, *after)


def transposed_kernel(f_hbm, z_all, p_all, x_two, r2, r3, r1, g_hbm, *refs):
    out, mine, other, fbuf, pr, pc, acc, g, tbuf, flat, s_f, s_in, s_out = refs[-13:]
    x, yh = lax.axis_index("x"), lax.axis_index("yh")
    z, yl, c = lax.axis_index("z"), lax.axis_index("yl"), lax.axis_index("c")
    y = yh * 2 + yl

    def f_copies(s):
        made = []
        for j in range(4):
            a = lax.rem(yh + j % 2, 2) * 4 + lax.rem(x + 2 * s + j // 2, 4)
            made.append(pltpu.make_async_copy(band(f_hbm, a), fbuf.at[s, pl.ds(j * U, U)], s_f.at[s, j]))
        return made

    first = []
    for k in range(4):
        zs = lax.rem(z + 4 - k, 4)
        for m, yb in ((0, yl), (1, 1 - yl)):
            first.append(((yb * 4 + zs) * 2 + c, z_all.at[k, m]))
            first.append(((yb * 4 + zs) * 2 + 1 - c, p_all.at[k, m]))
    ins = [pltpu.make_async_copy(src, band(pr, a), s_in.at[i]) for i, (a, src) in enumerate(first)]
    local_rows = {0: x_two}
    for k, r in zip(NEAR, (r2, r3, r1)):
        local_rows[4 - k] = r
    late = [
        pltpu.make_async_copy(r.at[m], band(pc, 2 * k + m), s_in.at[16 + 2 * k + m])
        for k, r in local_rows.items()
        for m in (0, 1)
    ]
    late.append(pltpu.make_async_copy(g_hbm, g, s_in.at[24]))
    for cp in f_copies(0) + ins:
        cp.start()
    acc[...] = jnp.zeros_like(acc)
    for cp in ins:
        cp.wait()
    for cp in late:
        cp.start()

    def out_copy(k):
        return pltpu.make_async_copy(tbuf.at[k], out.at[k], s_out.at[k])

    def step(s, _):
        @pl.when(s == 0)
        def _():
            for cp in f_copies(1):
                cp.start()

        for cp in f_copies(s):
            cp.wait()
        t = jnp.dot(fbuf[s], pr[...], preferred_element_type=f32)
        for j in range(4):
            tbuf[2 * s + j // 2, j % 2] = t[j * U : (j + 1) * U]
        out_copy(2 * s).start()
        out_copy(2 * s + 1).start()

        @pl.when(s == 0)
        def _():
            for cp in late:
                cp.wait()

        hi = t.astype(bf16)
        lo = (t - hi.astype(f32)).astype(bf16)
        p = pc[pl.ds(pl.multiple_of(s * 4 * U, 4 * U), 4 * U), :]
        acc[...] += lax.dot_general(p, hi, DIM0, preferred_element_type=f32) + lax.dot_general(
            p, lo, DIM0, preferred_element_type=f32
        )
        return 0

    lax.fori_loop(0, 2, step, 0)
    for n, (i, j) in enumerate(LOWER):
        flat[n * BLK : (n + 1) * BLK, :] = block(g, i, j) - block(acc, i, j) - block(acc, j, i).T
    for k, q in enumerate(chunk_order(y)):
        mine[k] = flat[pl.ds(pl.multiple_of((c * 4 + q) * CH, CH), CH), :]
        other[k] = flat[pl.ds(pl.multiple_of(((1 - c) * 4 + q) * CH, CH), CH), :]
    for k in range(4):
        out_copy(k).wait()


def transposed(flip, z_all, p_all, x_two, xr, g, *after):
    return pl.pallas_call(
        transposed_kernel,
        in_specs=[ANY] * (8 + len(after)),
        out_specs=[ANY, whole(), whole()],
        scratch_shapes=[
            pltpu.VMEM((2, 4 * U, 16 * U), bf16),
            pltpu.VMEM((16 * U, B), bf16),
            pltpu.VMEM((8 * U, B), bf16),
            pltpu.VMEM((B, B), f32),
            pltpu.VMEM((B, B), f32),
            pltpu.VMEM((4, 2, U, B), f32),
            pltpu.VMEM((8 * CH, BLK), f32),
            pltpu.SemaphoreType.DMA((2, 4)),
            pltpu.SemaphoreType.DMA((25,)),
            pltpu.SemaphoreType.DMA((4,)),
        ],
        out_shape=[
            jax.ShapeDtypeStruct((4, 2, U, B), f32),
            jax.ShapeDtypeStruct((4, CH, BLK), f32),
            jax.ShapeDtypeStruct((4, CH, BLK), f32),
        ],
        compiler_params=params(),
        cost_estimate=pl.CostEstimate(flops=15_000_000_000, bytes_accessed=17_000_000, transcendentals=0),
        name="transposed",
    )(flip, z_all, p_all, x_two, *xr, g, *after)


def cat(parts, axis):
    return parts[0] if len(parts) == 1 else jnp.concatenate(parts, axis=axis)


def halves(ref, *at):
    return ref[(0, *at)], ref[(1, *at)]


def cat2(pairs, axis):
    return cat([p[0] for p in pairs], axis), cat([p[1] for p in pairs], axis)


def dot3(a, b):
    return jnp.dot(cat([a[0], a[0], a[1]], 1), cat([b[0], b[1], b[0]], 0), preferred_element_type=f32)


def tail_kernel(mine, other, step_n, step_t, low_t, dg_ref, *refs):
    out_ref, flat = refs[-2:]
    c, y = lax.axis_index("c"), lax.axis_index("yh") * 2 + lax.axis_index("yl")
    for k, q in enumerate(chunk_order(y)):
        flat[pl.ds(pl.multiple_of((c * 4 + q) * CH, CH), CH), :] = mine[k]
        flat[pl.ds(pl.multiple_of(((1 - c) * 4 + q) * CH, CH), CH), :] = other[k]
    rows, cols = iotas(BLK)
    tri = rows >= cols
    q = {ij: flat[n * BLK : (n + 1) * BLK, :] for n, ij in enumerate(LOWER)}
    acc = {i: cat([q[i, j] for j in range(i + 1)], 1) for i in range(NB)}
    new = {}
    for i in reversed(range(NB)):
        both = dot3(halves(step_t, slice(0, (i + 1) * BLK), slice(i * BLK, (i + 1) * BLK)), split(acc[i]))
        con = both[i * BLK :]
        for r in range(i):
            acc[r] = acc[r] - both[r * BLK : (r + 1) * BLK, : (r + 1) * BLK]
        n = dg_ref[i * BLK : (i + 1) * BLK, : (i + 1) * BLK] - con
        corner = jnp.where(tri, n[:, i * BLK :], 0.0)
        new[i] = split(corner if i == 0 else cat([n[:, : i * BLK], corner], 1))
    keep = jnp.where(rows > cols, 1.0, jnp.where(rows == cols, 0.5, 0.0))
    inner = {}
    for i in range(NB):
        width = (i + 1) * BLK
        r = dot3(
            halves(low_t, slice(i * BLK, (i + 1) * BLK), slice(i * BLK, B)),
            cat2([tuple(v[:, :width] for v in new[k]) for k in range(i, NB)], 0),
        )
        parts = [] if i == 0 else [r[:, : i * BLK]]
        parts.append(r[:, i * BLK :] * keep)
        if width < B:
            parts.append(jnp.zeros((BLK, B - width), f32))
        inner[i] = cat(parts, 1)
    left = {}
    for i in reversed(range(NB)):
        both = dot3(halves(step_t, slice(0, (i + 1) * BLK), slice(i * BLK, (i + 1) * BLK)), split(inner[i]))
        left[i] = both[i * BLK :]
        for r in range(i):
            inner[r] = inner[r] - both[r * BLK : (r + 1) * BLK]
    acc = cat([left[i] for i in range(NB)], 0)
    right = {}
    for j in reversed(range(NB)):
        both = dot3(split(acc[:, j * BLK :]), halves(step_n, slice(j * BLK, (j + 1) * BLK), slice(0, (j + 1) * BLK)))
        right[j] = both[:, j * BLK :]
        if j:
            acc = acc[:, : j * BLK] - both[:, : j * BLK]
    for i in range(NB):
        for j in range(i + 1):
            v = 0.5 * (right[j][i * BLK : (i + 1) * BLK] + right[i][j * BLK : (j + 1) * BLK].T)
            out_ref[i * BLK : (i + 1) * BLK, j * BLK : (j + 1) * BLK] = v
            if i != j:
                out_ref[j * BLK : (j + 1) * BLK, i * BLK : (i + 1) * BLK] = v.T


def tail(mine, other, factor, diag_grad, *after):
    return pl.pallas_call(
        tail_kernel,
        out_shape=jax.ShapeDtypeStruct((B, B), f32),
        in_specs=[whole()] * 6 + [ANY] * len(after),
        out_specs=whole(),
        scratch_shapes=[pltpu.VMEM((8 * CH, BLK), f32)],
        compiler_params=params(),
        cost_estimate=pl.CostEstimate(flops=8_000_000_000, bytes_accessed=5_000_000, transcendentals=0),
        name="tail",
    )(mine, other, *factor, diag_grad, *after)


def solve_kernel(r_ref, d_ref, t_ref, step_n, out_ref):
    acc = r_ref[...] - d_ref[...] - t_ref[...]
    for j in reversed(range(NB)):
        both = dot3(split(acc[:, j * BLK :]), halves(step_n, slice(j * BLK, (j + 1) * BLK), slice(0, (j + 1) * BLK)))
        out_ref[:, j * BLK : (j + 1) * BLK] = both[:, j * BLK :]
        if j:
            acc = acc[:, : j * BLK] - both[:, : j * BLK]


def solve(r, d, t, step_n):
    return pl.pallas_call(
        solve_kernel,
        out_shape=jax.ShapeDtypeStruct((U, B), f32),
        in_specs=[whole()] * 4,
        out_specs=whole(),
        compiler_params=params(),
        cost_estimate=pl.CostEstimate(flops=1_000_000_000, bytes_accessed=3_000_000, transcendentals=0),
        name="solve",
    )(r, d, t, step_n)


def on_device(trailing_grad, panel, panel_grad, diag_factor, diag_grad):
    flip = trailing_grad.reshape(-1, trailing_grad.shape[3])

    x_swp = shift(panel, "yh", 1, 2)
    z_swp = shift(panel, "yl", 1, 2)
    *factor, g = prep(diag_factor, panel_grad, panel)
    x_swp, z_swp = after(x_swp, g), after(z_swp, g)
    x_two = jnp.stack([panel, x_swp])
    z_two = jnp.stack([panel, after(z_swp, x_two)])
    z_recv = [shift(z_two, "z", k) for k in NEAR]
    x_recv = [shift(x_two, "x", k) for k in NEAR]
    z_recv, x_recv = lax.optimization_barrier((z_recv, x_recv))
    z_all = jnp.stack([z_two, z_recv[2], z_recv[0], z_recv[1]])
    p_all = shift(z_all, "c", 1, 2)

    half = lambda v: (v * 64.0).astype(f16)
    full = lambda v: v.astype(f32) * (1 / 64.0)

    t_all, q_mine, q_other = transposed(flip, z_all, p_all, x_two, x_recv, g)
    t_out = {k: half(t_all[k]) for k in NEAR}
    t_in = {k: shift(t_out[k], "x", k) for k in NEAR}
    q_pair = shift(after(q_other, *t_out.values()), "c", 1, 2)
    y_axis = ("yh", "yl")
    two = q_mine[:2] + q_pair[:2] + swap(q_mine[2:] + q_pair[2:], y_axis, False)
    part = two[0] + swap(two[1], y_axis, True)
    t_sum = after(t_all[0] + (full(t_in[2]) + full(t_in[3]) + full(t_in[1])))
    t_last = shift(t_sum[1], "yh", 1, 2)
    x_two = after(x_two, part, t_in[1], t_in[3])
    d_mine, d_other = direct(flip, x_two, x_recv)
    d_pair = shift(d_other, "c", 1, 2)
    for far in (False, True):
        part = part + swap(part, "z", far)
    d_pair = after(d_pair, part)
    d_own = d_mine[0] + d_pair[0]
    d_out = {k: half(d_mine[k] + d_pair[k]) for k in NEAR}
    d_in = {k: shift(d_out[k], "z", k) for k in NEAR}
    part = after(part, *d_out.values())
    part = after(part + swap(part, "x", False), t_sum)
    part = part + swap(part, "x", True)
    part = after(part, d_in[1], d_in[3])
    two = after(jnp.stack([part, swap(part, y_axis, True)]), t_last)
    q_all = jnp.concatenate([two, swap(two, y_axis, False)])
    d_far = d_own[1] + (full(d_in[2][1]) + full(d_in[3][1]) + full(d_in[1][1]))
    d_last = shift(d_far, "yl", 1, 2)
    near = (
        panel_grad
        - t_sum[0]
        - (d_own[0] + (full(d_in[2][0]) + full(d_in[3][0]) + full(d_in[1][0])))
    )
    q_pair = after(shift(q_all, "c", 1, 2), d_far)
    diag_adj = tail(q_all, q_pair, factor, diag_grad)
    near = after(near, diag_adj)
    return solve(near, d_last, t_last, factor[0]), diag_adj


def solution(mesh):
    fine = Mesh(mesh.devices.reshape(2, 4, 2, 4, 2), ("yh", "x", "yl", "z", "c"))
    row, col = ("yh", "x"), ("yl", "z", "c")
    return jax.shard_map(
        on_device,
        mesh=fine,
        in_specs=(P(None, col, None, row), P(row + col, None), P(row + col, None), P(), P()),
        out_specs=(P(row + col, None), P()),
        check_vma=False,
    )
```
